256 devices in a mesh: rep: 64 (over y, z, x_hi), fsdp: 4 (over x_lo, core).
Axes of the slice: x: 4 (x_hi: 2, x_lo: 2; x = x_hi * 2 + x_lo), y: 4, z: 8, core: 2. Of those that a mesh axis runs over, the one named last changes fastest.
Arguments:
- local_weights: bfloat16 [64, 2, 1024, 4096], P('rep', None, 'fsdp'), may hold values from -16 to 16
- outer_weights: bfloat16 [2, 1024, 4096], P(None, 'fsdp'), may hold values from -6 to 6
- momentum: float32 [2, 1024, 4096], P(None, 'fsdp', 'rep'), may hold values from -6 to 6
- swa_mean: float32 [2, 1024, 4096], P(None, 'fsdp', 'rep'), may hold values from -6 to 6
- token_counts: int32 [64], P('rep'), may hold values from 262144 to 4194304, as said below
- swa_step: int32 [1], replicated, may hold values from 1 to 7
Outputs:
- new_weights: bfloat16 [2, 1024, 4096], P(None, 'fsdp')
- new_momentum: float32 [2, 1024, 4096], P(None, 'fsdp', 'rep')
- new_swa: float32 [2, 1024, 4096], P(None, 'fsdp', 'rep')
The draws below stay inside these ranges and needn't reach their ends.
Inputs may be any that keep to these rules, and one draw needn't show every extreme that they name: `token_counts`: exactly one replica holds the largest count, 4194304 tokens; every other replica holds fewer.
All inputs are finite; a program needn't handle non-finite values.
Results may differ from the reference program's by a relative error of at most 0.0004.
Values may be sent and summed in bfloat16 or wider, within the bound.
A program may use at most 128 MiB of HBM per device.

```python
import jax
import jax.numpy as jnp
from jax import lax

D = 4096
KVW = 1024
MATS = 2
REPLICAS = 64


def draw_token_counts(key, part):
    key = jax.random.fold_in(key, 11)
    key_jitter, key_common, key_top = jax.random.split(key, 3)
    index = jnp.arange(REPLICAS, dtype=jnp.int32)
    ramp = 262144 + index * 1310720 // REPLICAS
    jitter = jax.random.randint(key_jitter, (REPLICAS,), 0, 524288, dtype=jnp.int32)
    common = jax.random.randint(key_common, (), 0, 524288, dtype=jnp.int32)
    top_index = jax.random.randint(key_top, (), 0, REPLICAS, dtype=jnp.int32)
    others = index != top_index
    counts = jnp.where(others, ramp + jitter + common, jnp.full((), 4194304, jnp.int32))
    return counts.astype(jnp.int32)


def raised(result, stream_key, source, target, shards_of, factor):
    def block_of(dim):
        return (jnp.arange(result.shape[dim]) // (result.shape[dim] // shards_of)).reshape((-1,) + (1,) * (result.ndim - 1 - dim))

    first = jax.random.permutation(stream_key, shards_of)[block_of(target)]
    second = (block_of(target) + shards_of // 2) % shards_of
    return jnp.where((block_of(source) == first) | (block_of(source) == second), factor * result, result)


def steps_of(key, shape, pieces, smallest, largest):
    gain, own = 1.0, jax.random.fold_in(key, 6)
    for position, shards_of in pieces:
        draws = jnp.exp(jax.random.uniform(jax.random.fold_in(own, position), (shards_of,), jnp.float32, smallest / len(pieces), largest / len(pieces)))
        gain = gain * jnp.repeat(draws, shape[position] // shards_of).reshape([-1 if axis == position else 1 for axis in range(len(shape))])
    return gain


def bell_draw(key, extent, spread, bound, cuts=(), held_as=jnp.bfloat16):
    result = jax.random.normal(key, extent, jnp.float32) * spread
    if len(cuts) > 0:
        result = steps_of(key, extent, cuts, -0.22, 0.18) * result
    return jnp.clip(result, min=-bound, max=bound).astype(held_as)


def gaussian_with(own_key, shape, spread, most, pieces, heavy, kind=jnp.bfloat16):
    drawn = spread * jax.random.normal(own_key, shape, jnp.float32)
    if pieces:
        drawn = drawn * steps_of(own_key, shape, pieces, -0.22, 0.18)
    return jnp.clip(raised(drawn, jax.random.fold_in(own_key, 3), *heavy), -most, most).astype(kind)


def setup_inputs(seed: int = 0) -> dict:
    key_of = jax.random.split(jax.random.key(seed), 7)
    return {
        "local_weights": gaussian_with(key_of[0], (REPLICAS, MATS, KVW, D), 1.0, 16.0, ((0, 64), (2, 4)), (0, 3, 64, 4.0)),
        "outer_weights": bell_draw(key_of[1], (MATS, KVW, D), 1.0, 6.0, ((1, 4),)),
        "momentum": bell_draw(key_of[2], (MATS, KVW, D), 1.0, 6.0, ((1, 4), (2, 64)), jnp.float32),
        "swa_mean": bell_draw(key_of[3], (MATS, KVW, D), 1.0, 6.0, ((1, 4), (2, 64)), jnp.float32),
        "token_counts": draw_token_counts(jax.random.fold_in(key_of[6], 71), 0),
        "swa_step": jax.random.randint(key_of[5], (1,), 1, 8).astype(jnp.int32),
    }


def reference(local_weights, outer_weights, momentum, swa_mean, token_counts, swa_step):
    total = jnp.sum(token_counts).astype(jnp.int32)
    shares = token_counts.astype(jnp.float32) / total.astype(jnp.float32)
    outer = outer_weights.astype(jnp.float32)

    def accumulate(acc, item):
        piece, share = item
        return acc + share * (outer - piece.astype(jnp.float32)), None

    pseudo_grad, _ = lax.scan(accumulate, jnp.zeros(outer.shape, jnp.float32), (local_weights, shares))
    new_momentum = 0.9 * momentum + pseudo_grad
    updated = outer - 0.7 * (pseudo_grad + 0.9 * new_momentum)
    new_weights = updated.astype(jnp.bfloat16)
    divisor = swa_step[0].astype(jnp.float32) + 1.0
    new_swa = swa_mean + (updated - swa_mean) / divisor
    return new_weights, new_momentum, new_swa
```

```python
import functools

import jax
import jax.numpy as jnp
from jax import lax
from jax.experimental import pallas as pl
from jax.experimental.pallas import tpu as pltpu
from jax.sharding import PartitionSpec as P

MESH = pl.DeviceIdType.MESH
NY, NZ, NX = 4, 8, 2
LANES = 128
R = 16
AHEAD = 3


def kernel(
    na, nd, rows,
    local, outer, mom_t, swa_t, tokens, step_no,
    out, nmom_t, nswa_t,
    a_raw, a_own, a_out, a_p, a_l, a_s, a_q, a_qx, a_w, a_wx, a_stage,
    d_raw, d_own, d_out, d_p, d_l, d_s, d_q, d_qy, d_w, d_stage,
    cnt, cnt_z, cnt_x, total, mbuf, sbuf, mfull, sfull, ofull, mback, sback,
    a_ss, a_rs, d_ss, d_rs, c_ss, c_rs, m_ss, m_rs, l_sem, o_sem,
):
    f32, bf16 = jnp.float32, jnp.bfloat16
    rep, fsdp = lax.axis_index("rep"), lax.axis_index("fsdp")
    y, z, x = rep // (NZ * NX), (rep // NX) % NZ, rep % NX
    other = 1 - x
    d_first = na * R

    def at(yy, zz, xx):
        return ((lax.rem(yy + 2 * NY, NY) * NZ + lax.rem(zz + 2 * NZ, NZ)) * NX + xx, fsdp)

    def zi(k):
        return lax.rem(z + k + 2 * NZ, NZ)

    def yi(k):
        return lax.rem(y + k + 2 * NY, NY)

    def remote(src, dst, ss, rs, where):
        return pltpu.make_async_remote_copy(
            src_ref=src, dst_ref=dst, send_sem=ss, recv_sem=rs, device_id=where, device_id_type=MESH
        )

    partner = at(y, z, other)
    y_peers = [at(y + k, z, x) for k in range(1, NY)]
    z_peers = [at(y, z + k, x) for k in range(1, NZ)]

    def a_rows(c):
        return pl.ds(pl.multiple_of(c * R, R), R)

    def d_rows(c):
        return pl.ds(pl.multiple_of(d_first + c * R, R), R)

    def count_y(k):
        return remote(cnt.at[0], cnt.at[k], c_ss.at[k], c_rs.at[k], y_peers[k - 1])

    def count_own_x():
        return remote(cnt.at[0], cnt.at[NY], c_ss.at[0], c_rs.at[0], partner)

    def count_z(k):
        return remote(cnt_z.at[0], cnt_z.at[k], c_ss.at[NY + k], c_rs.at[NY + k], z_peers[k - 1])

    def count_x():
        return remote(cnt_x.at[0], cnt_x.at[1], c_ss.at[NY], c_rs.at[NY], partner)

    half = pl.ds(pl.multiple_of(x * 64, 64), 64)
    other_half = pl.ds(pl.multiple_of(other * 64, 64), 64)

    def mom_in():
        return remote(mom_t.at[other], mbuf.at[half], m_ss.at[0], m_rs.at[0], partner)

    def swa_in():
        return remote(swa_t.at[other], sbuf.at[half], m_ss.at[1], m_rs.at[1], partner)

    def mom_back():
        return remote(mbuf.at[other_half], mback, m_ss.at[2], m_rs.at[2], partner)

    def swa_back():
        return remote(sbuf.at[other_half], sback, m_ss.at[3], m_rs.at[3], partner)

    ycols = pl.ds(pl.multiple_of(y * (NZ * LANES), NZ * LANES), NZ * LANES)
    cols = pl.ds(pl.multiple_of((y * NZ + z) * LANES, LANES), LANES)
    arows = pl.ds(0, na * R)
    drows = pl.ds(d_first, nd * R)
    loads = [
        pltpu.make_async_copy(outer.at[x, :, cols], ofull, l_sem.at[0]),
    ]
    if na:
        loads += [
            pltpu.make_async_copy(local.at[0, :, arows, ycols], a_own, l_sem.at[1]),
            pltpu.make_async_copy(outer.at[:, arows, ycols], a_out, l_sem.at[2]),
        ]
    if nd:
        loads += [
            pltpu.make_async_copy(local.at[0, x, drows, :], d_own, l_sem.at[3]),
            pltpu.make_async_copy(outer.at[x, drows, :], d_out, l_sem.at[4]),
        ]
    for load in loads:
        load.start()
    cnt[0] = jnp.full((8, LANES), tokens[0], jnp.int32)

    barrier = pltpu.get_barrier_semaphore()
    peers = y_peers + z_peers + [partner]
    for peer in peers:
        pl.semaphore_signal(barrier, inc=1, device_id=peer, device_id_type=MESH)
    pl.semaphore_wait(barrier, len(peers))

    def a_first(c, k):
        theirs = pl.ds(pl.multiple_of(yi(k) * (NZ * LANES), NZ * LANES), NZ * LANES)
        return remote(
            local.at[0, :, a_rows(c), theirs], a_raw.at[c, k - 1], a_ss.at[c, k - 1], a_rs.at[c, k - 1], y_peers[k - 1]
        )

    def d_first_copy(c):
        return remote(local.at[0, other, d_rows(c), :], d_raw.at[c], d_ss.at[c, 0], d_rs.at[c, 0], partner)

    def sums_up(c, sign, p, long, short, ss, rs, base):
        def way_l(k):
            src = p.at[c, zi(4 * sign)] if k == 0 else long.at[c, k - 1]
            return remote(src, long.at[c, k], ss.at[c, base + k], rs.at[c, base + k], at(y, z + sign, x))

        def way_s(k):
            src = p.at[c, zi(-3 * sign)] if k == 0 else short.at[c, k - 1]
            return remote(src, short.at[c, k], ss.at[c, base + 4 + k], rs.at[c, base + 4 + k], at(y, z - sign, x))

        return way_l, way_s

    def spread(c, sign, blocks, ss, rs, base):
        def way_l(k):
            block = blocks(c, zi(-k * sign))
            return remote(block, block, ss.at[c, base + k], rs.at[c, base + k], at(y, z + sign, x))

        def way_s(k):
            block = blocks(c, zi(k * sign))
            return remote(block, block, ss.at[c, base + 4 + k], rs.at[c, base + 4 + k], at(y, z - sign, x))

        def into_l(k):
            block = blocks(c, zi(-(k + 1) * sign))
            return remote(block, block, ss.at[c, base + k], rs.at[c, base + k], at(y, z + sign, x))

        def into_s(k):
            block = blocks(c, zi((k + 1) * sign))
            return remote(block, block, ss.at[c, base + 4 + k], rs.at[c, base + 4 + k], at(y, z - sign, x))

        return way_l, way_s, into_l, into_s

    def update(rws, pg_sum):
        o = ofull[rws, :].astype(f32)
        pg = pg_sum / total[0:1, :]
        nm = 0.9 * mfull[rws, :] + pg
        upd = o - 0.7 * (pg + 0.9 * nm)
        s = sfull[rws, :]
        divisor = step_no[0].astype(f32) + 1.0
        mfull[rws, :] = nm
        sfull[rws, :] = s + (upd - s) / divisor
        return upd.astype(bf16)

    def ring_stage(kind, stage, c, sign, p, long, short, ss, rs, base):
        way_l, way_s = sums_up(c, sign, p, long, short, ss, rs, base)
        if stage == 0:
            way_l(0).start()
            way_s(0).start()
            return
        k = stage - 1
        way_l(k).wait()
        if k < 3:
            long[c, k] += p[c, zi((3 - k) * sign)]
            way_l(k + 1).start()
            way_s(k).wait()
            if k < 2:
                short[c, k] += p[c, zi(-(2 - k) * sign)]
                way_s(k + 1).start()

    def spread_stage(stage, c, sign, blocks, ss, rs, base):
        way_l, way_s, into_l, into_s = spread(c, sign, blocks, ss, rs, base)
        if stage > 0:
            k = stage - 1
            into_l(k).wait_recv()
            if k < 3:
                into_s(k).wait_recv()
        if stage < 4:
            way_l(stage).start()
            if stage < 3:
                way_s(stage).start()
        if stage > 0:
            k = stage - 1
            way_l(k).wait_send()
            if k < 3:
                way_s(k).wait_send()

    def a_blocks(c, zz):
        return a_w.at[c, zz]

    def a_mid(c):
        return remote(a_q.at[c, other], a_qx.at[c], a_ss.at[c, 10], a_rs.at[c, 10], partner)

    def a_wy(c, k):
        mine = a_w.at[c, z, y]
        return remote(mine, mine, a_ss.at[c, 10 + k], a_rs.at[c, 10 + k], y_peers[k - 1])

    def a_wy_into(c, k):
        theirs = a_w.at[c, z, yi(-k)]
        return remote(theirs, theirs, a_ss.at[c, 10 + k], a_rs.at[c, 10 + k], y_peers[k - 1])

    def a_last(c):
        return remote(a_w.at[c], a_wx.at[c], a_ss.at[c, 21], a_rs.at[c, 21], partner)

    def a_store(c, m):
        return pltpu.make_async_copy(a_stage.at[c, m], out.at[m, a_rows(c), :], o_sem.at[c, m])

    def a_stage_fn(stage, c):
        sign = 1 - 2 * (c % 2)
        ring = functools.partial(ring_stage, "a", c=c, sign=sign, p=a_p, long=a_l, short=a_s, ss=a_ss, rs=a_rs, base=3)
        out_ring = functools.partial(spread_stage, c=c, sign=sign, blocks=a_blocks, ss=a_ss, rs=a_rs, base=14)
        if stage == 0:
            for k in range(1, NY):
                a_first(c, k).wait()
            for zz in range(NZ):
                sl = pl.ds(zz * LANES, LANES)
                for m in range(2):
                    o = a_out[m, a_rows(c), sl].astype(f32)
                    acc = cnt_f(0) * (o - a_own[m, a_rows(c), sl].astype(f32))
                    for k in range(1, NY):
                        acc += cnt_f(k) * (o - a_raw[c, k - 1, m, :, sl].astype(f32))
                    a_p[c, zz, m] = acc
            ring(0)
        elif stage <= 3:
            ring(stage)
        elif stage == 4:
            ring(4)
            a_q[c] = a_p[c, z] + a_l[c, 3] + a_s[c, 2]
            a_mid(c).start()
        elif stage == 5:
            a_mid(c).wait()
            a_w[c, z, y] = update(a_rows(c), a_q[c, x] + a_qx[c])
            for k in range(1, NY):
                a_wy(c, k).start()
        elif stage == 6:
            for k in range(1, NY):
                a_wy_into(c, k).wait_recv()
            out_ring(0)
            for k in range(1, NY):
                a_wy(c, k).wait_send()
        elif stage <= 9:
            out_ring(stage - 6)
        elif stage == 10:
            out_ring(4)
            a_last(c).start()
            for yy in range(NY):
                for zz in range(NZ):
                    a_stage[c, x, :, pl.ds((yy * NZ + zz) * LANES, LANES)] = a_w[c, zz, yy]
            a_store(c, x).start()
        else:
            a_last(c).wait()
            for yy in range(NY):
                for zz in range(NZ):
                    a_stage[c, other, :, pl.ds((yy * NZ + zz) * LANES, LANES)] = a_wx[c, zz, yy]
            a_store(c, other).start()

    def d_blocks(c, zz):
        return d_w.at[c, y, zz]

    def d_mid(c, k):
        return remote(d_q.at[c, yi(k)], d_qy.at[c, k - 1], d_ss.at[c, 7 + k], d_rs.at[c, 7 + k], y_peers[k - 1])

    def d_wx(c):
        mine = d_w.at[c, y, z, x]
        return remote(mine, mine, d_ss.at[c, 11], d_rs.at[c, 11], partner)

    def d_wx_into(c):
        theirs = d_w.at[c, y, z, other]
        return remote(theirs, theirs, d_ss.at[c, 11], d_rs.at[c, 11], partner)

    def d_last(c, k):
        mine = d_w.at[c, y]
        return remote(mine, mine, d_ss.at[c, 18 + k], d_rs.at[c, 18 + k], y_peers[k - 1])

    def d_last_into(c, k):
        theirs = d_w.at[c, yi(-k)]
        return remote(theirs, theirs, d_ss.at[c, 18 + k], d_rs.at[c, 18 + k], y_peers[k - 1])

    def d_store(c):
        return pltpu.make_async_copy(d_stage.at[c], out.at[:, d_rows(c), :], o_sem.at[na + c, 0])

    def d_stage_fn(stage, c):
        sign = 2 * (c % 2) - 1
        ring = functools.partial(ring_stage, "d", c=c, sign=sign, p=d_p, long=d_l, short=d_s, ss=d_ss, rs=d_rs, base=1)
        out_ring = functools.partial(spread_stage, c=c, sign=sign, blocks=d_blocks, ss=d_ss, rs=d_rs, base=12)
        if stage == 0:
            d_first_copy(c).wait()
            own = pl.ds(pl.multiple_of(c * R, R), R)
            for yy in range(NY):
                for zz in range(NZ):
                    sl = pl.ds((yy * NZ + zz) * LANES, LANES)
                    o = d_out[own, sl].astype(f32)
                    mine = cnt_f(0) * (o - d_own[own, sl].astype(f32))
                    d_p[c, zz, yy] = mine + cnt_f(NY) * (o - d_raw[c, :, sl].astype(f32))
            ring(0)
        elif stage <= 3:
            ring(stage)
        elif stage == 4:
            ring(4)
            d_q[c] = d_p[c, z] + d_l[c, 3] + d_s[c, 2]
            for k in range(1, NY):
                d_mid(c, k).start()
        elif stage == 5:
            for k in range(1, NY):
                d_mid(c, k).wait()
            d_w[c, y, z, x] = update(d_rows(c), d_q[c, y] + d_qy[c, 0] + d_qy[c, 1] + d_qy[c, 2])
            d_wx(c).start()
        elif stage == 6:
            d_wx_into(c).wait_recv()
            out_ring(0)
            d_wx(c).wait_send()
        elif stage <= 9:
            out_ring(stage - 6)
        elif stage == 10:
            out_ring(4)
            for k in range(1, NY):
                d_last(c, k).start()
        else:
            for k in range(1, NY):
                d_last_into(c, k).wait_recv()
            for yy in range(NY):
                for zz in range(NZ):
                    for m in range(2):
                        d_stage[c, m, :, pl.ds((yy * NZ + zz) * LANES, LANES)] = d_w[c, yy, zz, m]
            d_store(c).start()
            for k in range(1, NY):
                d_last(c, k).wait_send()

    def cnt_f(k):
        return cnt[k, 0:1, :].astype(f32)

    for k in range(1, NY):
        count_y(k).start()
    count_own_x().start()

    def send_first(c):
        if na:

            @pl.when(c < na)
            def _():
                for k in (2, 1, 3):
                    a_first(c, k).start()

        if nd:

            @pl.when(c < nd)
            def _():
                d_first_copy(c).start()

    for c in range(AHEAD):
        send_first(c)
    mom_in().start()
    swa_in().start()
    mbuf[half, :] = mom_t[x]
    sbuf[half, :] = swa_t[x]

    for k in range(1, NY):
        count_y(k).wait()
    count_own_x().wait()
    cnt_z[0] = cnt[0] + cnt[1] + cnt[2] + cnt[3]
    for k in range(1, NZ):
        count_z(k).start()
    for load in loads:
        load.wait()

    def slot(t, carry):
        @pl.when(t == 2)
        def _():
            for k in range(1, NZ):
                count_z(k).wait()
            acc = cnt_z[0]
            for k in range(1, NZ):
                acc += cnt_z[k]
            cnt_x[0] = acc
            count_x().start()

        @pl.when(t == 4)
        def _():
            count_x().wait()
            total[...] = (cnt_x[0] + cnt_x[1]).astype(f32)
            mom_in().wait()
            swa_in().wait()
            mfull[...] = mbuf[...].T
            sfull[...] = sbuf[...].T

        for stage in range(11, -1, -1):
            c = t - stage
            if na:
                pl.when((c >= 0) & (c < na))(functools.partial(a_stage_fn, stage, c))
            if nd:
                pl.when((c >= 0) & (c < nd))(functools.partial(d_stage_fn, stage, c))

        send_first(t + AHEAD)

        @pl.when(t == max(na, nd) + 5)
        def _():
            mbuf[...] = mfull[...].T
            sbuf[...] = sfull[...].T
            mom_back().start()
            swa_back().start()
            nmom_t[x] = mbuf[half, :]
            nswa_t[x] = sbuf[half, :]

        return carry

    lax.fori_loop(0, max(na, nd) + 11, slot, 0)
    mom_back().wait()
    swa_back().wait()
    nmom_t[other] = mback[...]
    nswa_t[other] = sback[...]

    def wait_out(c, carry):
        if na:

            @pl.when(c < na)
            def _():
                a_store(c, x).wait()
                a_store(c, other).wait()

        if nd:

            @pl.when(c < nd)
            def _():
                d_store(c).wait()

        return carry

    lax.fori_loop(0, max(na, nd), wait_out, 0)


def per_device(local, outer, momentum, swa, tokens, step_no):
    mats, rows, width = outer.shape
    na = rows // R // 2
    nd = rows // R - na
    f32, bf16, i32 = jnp.float32, jnp.bfloat16, jnp.int32
    vmem = pltpu.VMEM
    wide = NZ * LANES
    a, d = max(na, 1), max(nd, 1)
    scratch = [
        vmem((a, NY - 1, mats, R, wide), bf16),
        vmem((mats, a * R, wide), bf16),
        vmem((mats, a * R, wide), bf16),
        vmem((a, NZ, mats, R, LANES), f32),
        vmem((a, 4, mats, R, LANES), f32),
        vmem((a, 3, mats, R, LANES), f32),
        vmem((a, mats, R, LANES), f32),
        vmem((a, R, LANES), f32),
        vmem((a, NZ, NY, R, LANES), bf16),
        vmem((a, NZ, NY, R, LANES), bf16),
        vmem((a, mats, R, width), bf16),
        vmem((d, R, width), bf16),
        vmem((d * R, width), bf16),
        vmem((d * R, width), bf16),
        vmem((d, NZ, NY, R, LANES), f32),
        vmem((d, 4, NY, R, LANES), f32),
        vmem((d, 3, NY, R, LANES), f32),
        vmem((d, NY, R, LANES), f32),
        vmem((d, NY - 1, R, LANES), f32),
        vmem((d, NY, NZ, NX, R, LANES), bf16),
        vmem((d, mats, R, width), bf16),
        vmem((NY + 1, 8, LANES), i32),
        vmem((NZ, 8, LANES), i32),
        vmem((2, 8, LANES), i32),
        vmem((8, LANES), f32),
        vmem((LANES, rows), f32),
        vmem((LANES, rows), f32),
        vmem((rows, LANES), f32),
        vmem((rows, LANES), f32),
        vmem((rows, LANES), bf16),
        vmem((LANES // 2, rows), f32),
        vmem((LANES // 2, rows), f32),
        pltpu.SemaphoreType.DMA((a, 22)),
        pltpu.SemaphoreType.DMA((a, 22)),
        pltpu.SemaphoreType.DMA((d, 22)),
        pltpu.SemaphoreType.DMA((d, 22)),
        pltpu.SemaphoreType.DMA((NY + NZ,)),
        pltpu.SemaphoreType.DMA((NY + NZ,)),
        pltpu.SemaphoreType.DMA((4,)),
        pltpu.SemaphoreType.DMA((4,)),
        pltpu.SemaphoreType.DMA((5,)),
        pltpu.SemaphoreType.DMA((na + nd, 2)),
    ]
    anywhere = pl.BlockSpec(memory_space=pl.ANY)
    in_vmem = pl.BlockSpec(memory_space=pltpu.VMEM)
    in_smem = pl.BlockSpec(memory_space=pltpu.SMEM)
    turned = jax.ShapeDtypeStruct((mats, LANES // 2, rows), f32)
    new_weights, new_mom, new_swa = pl.pallas_call(
        functools.partial(kernel, na, nd, rows),
        out_shape=(jax.ShapeDtypeStruct(outer.shape, bf16), turned, turned),
        in_specs=[anywhere, anywhere, in_vmem, in_vmem, in_smem, in_smem],
        out_specs=(anywhere, in_vmem, in_vmem),
        scratch_shapes=scratch,
        compiler_params=pltpu.CompilerParams(
            collective_id=0, has_side_effects=True, vmem_limit_bytes=56 * 2**20
        ),
    )(local, outer, jnp.swapaxes(momentum, 1, 2), jnp.swapaxes(swa, 1, 2), tokens, step_no)
    return new_weights, jnp.swapaxes(new_mom, 1, 2), jnp.swapaxes(new_swa, 1, 2)


def solution(mesh):
    return jax.shard_map(
        per_device,
        mesh=mesh,
        in_specs=(
            P("rep", None, "fsdp", None),
            P(None, "fsdp", None),
            P(None, "fsdp", "rep"),
            P(None, "fsdp", "rep"),
            P("rep"),
            P(),
        ),
        out_specs=(P(None, "fsdp", None), P(None, "fsdp", "rep"), P(None, "fsdp", "rep")),
        check_vma=False,
    )
```

```python
import functools

import jax
import jax.numpy as jnp
from jax import lax
from jax.experimental import pallas as pl
from jax.experimental.pallas import tpu as pltpu
from jax.sharding import PartitionSpec as P

MESH = pl.DeviceIdType.MESH
NY, NZ, NX = 4, 8, 2
LANES = 128
R = 16
AHEAD = 3
A_AT = tuple(range(9))
D_AT = tuple(range(9))
ORDER = tuple((kind, stage) for stage in range(9) for kind in "AD")
RAW, RING, MID, FIRST, SECOND, LAST = 0, 1, 5, 6, 7, 8


def kernel(
    na, nd, rows,
    local, outer, mom_t, swa_t, tokens, step_no,
    out, nmom_t, nswa_t,
    a_raw, a_own, a_out, a_p, a_r, a_q, a_qx, a_w, a_wx, a_stage,
    d_raw, d_own, d_out, d_p, d_r, d_q, d_qy, d_w, d_stage,
    cnt, cnt_z, cnt_x, total, mbuf, sbuf, mfull, sfull, ofull,
    a_ss, a_rs, d_ss, d_rs, raw_ss, c_ss, c_rs, m_ss, m_rs, l_sem, o_sem,
):
    f32, bf16 = jnp.float32, jnp.bfloat16
    rep, fsdp = lax.axis_index("rep"), lax.axis_index("fsdp")
    y, z, x = rep // (NZ * NX), (rep // NX) % NZ, rep % NX
    other = 1 - x
    d_row = na * R

    def at(yy, zz, xx):
        return ((lax.rem(yy + 2 * NY, NY) * NZ + lax.rem(zz + 2 * NZ, NZ)) * NX + xx, fsdp)

    def zi(k):
        return lax.rem(z + k + 2 * NZ, NZ)

    def yi(k):
        return lax.rem(y + k + 2 * NY, NY)

    def send(src, dst, ss, rs, where):
        pltpu.make_async_remote_copy(
            src_ref=src, dst_ref=dst, send_sem=ss, recv_sem=rs, device_id=where, device_id_type=MESH
        ).start()

    def drain(ref, sem):
        pltpu.make_async_copy(ref, ref, sem).wait()

    partner = at(y, z, other)
    y_peers = [at(y + k, z, x) for k in range(1, NY)]
    z_peers = [at(y, z + k, x) for k in range(1, NZ)]

    def a_rows(c):
        return pl.ds(pl.multiple_of(c * R, R), R)

    def d_rows(c):
        return pl.ds(pl.multiple_of(d_row + c * R, R), R)

    def lanes(block):
        return pl.ds(block * LANES, LANES)

    def cnt_f(k):
        return cnt[k, 0:1, :].astype(f32)

    half = pl.ds(pl.multiple_of(x * (LANES // 2), LANES // 2), LANES // 2)
    other_half = pl.ds(pl.multiple_of(other * (LANES // 2), LANES // 2), LANES // 2)
    ycols = pl.ds(pl.multiple_of(y * (NZ * LANES), NZ * LANES), NZ * LANES)
    cols = pl.ds(pl.multiple_of((y * NZ + z) * LANES, LANES), LANES)
    arows, drows = pl.ds(0, na * R), pl.ds(d_row, nd * R)
    loads = [
        pltpu.make_async_copy(local.at[0, :, arows, ycols], a_own, l_sem.at[1]),
        pltpu.make_async_copy(outer.at[:, arows, ycols], a_out, l_sem.at[2]),
        pltpu.make_async_copy(local.at[0, x, drows, :], d_own, l_sem.at[3]),
        pltpu.make_async_copy(outer.at[x, drows, :], d_out, l_sem.at[4]),
    ]
    late_loads = [
        pltpu.make_async_copy(outer.at[x, :, cols], ofull, l_sem.at[0]),
        pltpu.make_async_copy(mom_t.at[x], mbuf.at[half], l_sem.at[5]),
        pltpu.make_async_copy(swa_t.at[x], sbuf.at[half], l_sem.at[6]),
    ]
    for load in loads + late_loads:
        load.start()
    cnt[0] = jnp.full((8, LANES), tokens[0], jnp.int32)

    barrier = pltpu.get_barrier_semaphore()
    peers = y_peers + z_peers + [partner]
    for peer in peers:
        pl.semaphore_signal(barrier, inc=1, device_id=peer, device_id_type=MESH)
    pl.semaphore_wait(barrier, len(peers))

    def send_raw(c):
        @pl.when(c < na)
        def _():
            for k in (2, 1, 3):
                theirs = pl.ds(pl.multiple_of(yi(k) * (NZ * LANES), NZ * LANES), NZ * LANES)
                send(
                    local.at[0, :, a_rows(c), theirs], a_raw.at[c, k - 1],
                    raw_ss.at[0, c % 4], a_rs.at[c, RAW], y_peers[k - 1],
                )

        @pl.when(c < nd)
        def _():
            send(local.at[0, other, d_rows(c), :], d_raw.at[c], raw_ss.at[1, c % 4], d_rs.at[c, RAW], partner)

    def ring_stage(stage, c, sign, p, r, ss, rs):
        up, down = at(y, z + sign, x), at(y, z - sign, x)

        def step(k, long, short):
            send(long, r.at[c, k, 0], ss.at[c % 2, RING + k], rs.at[c, RING + k], up)
            if k < 3:
                send(short, r.at[c, k, 1], ss.at[c % 2, RING + k], rs.at[c, RING + k], down)

        if stage == 0:
            step(0, p.at[c, zi(4 * sign)], p.at[c, zi(-3 * sign)])
            return
        k = stage - 1
        came = r.at[c, k] if k < 3 else r.at[c, k, 0]
        drain(came, rs.at[c, RING + k])
        if k < 3:
            r[c, k, 0] += p[c, zi((3 - k) * sign)]
            if k < 2:
                r[c, k, 1] += p[c, zi(-(2 - k) * sign)]
            step(k + 1, r.at[c, k, 0], r.at[c, k, 1])
        drain(came, ss.at[c % 2, RING + k])

    def update(rws, pg_sum):
        o = ofull[rws, :].astype(f32)
        pg = pg_sum / total[0:1, :]
        nm = 0.9 * mfull[rws, :] + pg
        upd = o - 0.7 * (pg + 0.9 * nm)
        s = sfull[rws, :]
        divisor = step_no[0].astype(f32) + 1.0
        mfull[rws, :] = nm
        sfull[rws, :] = s + (upd - s) / divisor
        return upd.astype(bf16)

    def a_store(c, m):
        return pltpu.make_async_copy(a_stage.at[c, m], out.at[m, a_rows(c), :], o_sem.at[c, m])

    def a_stage_fn(stage, c):
        ring = functools.partial(ring_stage, c=c, sign=1 - 2 * (c % 2), p=a_p, r=a_r, ss=a_ss, rs=a_rs)

        def sems(k):
            return a_ss.at[c % 2, k], a_rs.at[c, k]

        def landed(ref, k):
            drain(ref, a_rs.at[c, k])

        def left(ref, k):
            drain(ref, a_ss.at[c % 2, k])

        if stage == 0:
            landed(a_raw.at[c], RAW)
            for zz in range(NZ):
                for m in range(2):
                    o = a_out[m, a_rows(c), lanes(zz)].astype(f32)
                    acc = cnt_f(0) * (o - a_own[m, a_rows(c), lanes(zz)].astype(f32))
                    for k in range(1, NY):
                        acc += cnt_f(k) * (o - a_raw[c, k - 1, m, :, lanes(zz)].astype(f32))
                    a_p[c, zz, m] = acc
            ring(0)
            drain(a_raw.at[c], raw_ss.at[0, c % 4])
        elif stage <= 3:
            ring(stage)
        elif stage == 4:
            ring(4)
            a_q[c] = a_p[c, z] + a_r[c, 3, 0] + a_r[c, 2, 1]
            send(a_q.at[c, other], a_qx.at[c], *sems(MID), partner)
        elif stage == 5:
            landed(a_qx.at[c], MID)
            mine = a_w.at[c, y, z]
            mine[...] = update(a_rows(c), a_q[c, x] + a_qx[c])
            for k in (4, 3, 5, 2, 6, 1, 7):
                send(mine, mine, *sems(FIRST), z_peers[k - 1])
            left(a_qx.at[c], MID)
        elif stage == 6:
            landed(a_w.at[c, y, pl.ds(0, NZ - 1)], FIRST)
            mine = a_w.at[c, y]
            for k in (2, 1, 3):
                send(mine, mine, *sems(SECOND), y_peers[k - 1])
            left(a_w.at[c, y, pl.ds(0, NZ - 1)], FIRST)
        elif stage == 7:
            landed(a_w.at[c, pl.ds(0, NY - 1)], SECOND)
            send(a_w.at[c], a_wx.at[c], *sems(LAST), partner)
            for yy in range(NY):
                for zz in range(NZ):
                    a_stage[c, x, :, lanes(yy * NZ + zz)] = a_w[c, yy, zz]
            a_store(c, x).start()
            left(a_w.at[c, pl.ds(0, NY - 1)], SECOND)
        else:
            landed(a_wx.at[c], LAST)
            for yy in range(NY):
                for zz in range(NZ):
                    a_stage[c, other, :, lanes(yy * NZ + zz)] = a_wx[c, yy, zz]
            a_store(c, other).start()
            left(a_wx.at[c], LAST)

    def d_store(c):
        return pltpu.make_async_copy(d_stage.at[c], out.at[:, d_rows(c), :], o_sem.at[na + c, 0])

    def d_stage_fn(stage, c):
        ring = functools.partial(ring_stage, c=c, sign=2 * (c % 2) - 1, p=d_p, r=d_r, ss=d_ss, rs=d_rs)

        def sems(k):
            return d_ss.at[c % 2, k], d_rs.at[c, k]

        def landed(ref, k):
            drain(ref, d_rs.at[c, k])

        def left(ref, k):
            drain(ref, d_ss.at[c % 2, k])

        if stage == 0:
            landed(d_raw.at[c], RAW)
            own = pl.ds(pl.multiple_of(c * R, R), R)
            for yy in range(NY):
                for zz in range(NZ):
                    sl = lanes(yy * NZ + zz)
                    o = d_out[own, sl].astype(f32)
                    mine = cnt_f(0) * (o - d_own[own, sl].astype(f32))
                    d_p[c, zz, yy] = mine + cnt_f(NY) * (o - d_raw[c, :, sl].astype(f32))
            ring(0)
            drain(d_raw.at[c], raw_ss.at[1, c % 4])
        elif stage <= 3:
            ring(stage)
        elif stage == 4:
            ring(4)
            d_q[c] = d_p[c, z] + d_r[c, 3, 0] + d_r[c, 2, 1]
            for k in (2, 1, 3):
                send(d_q.at[c, yi(k)], d_qy.at[c, k - 1], *sems(MID), y_peers[k - 1])
        elif stage == 5:
            landed(d_qy.at[c], MID)
            mine = d_w.at[c, y, x, z]
            mine[...] = update(d_rows(c), d_q[c, y] + d_qy[c, 0] + d_qy[c, 1] + d_qy[c, 2])
            for k in (4, 3, 5, 2, 6, 1, 7):
                send(mine, mine, *sems(FIRST), z_peers[k - 1])
            left(d_qy.at[c], MID)
        elif stage == 6:
            landed(d_w.at[c, y, x, pl.ds(0, NZ - 1)], FIRST)
            mine = d_w.at[c, y, x]
            send(mine, mine, *sems(SECOND), partner)
            left(d_w.at[c, y, x, pl.ds(0, NZ - 1)], FIRST)
        elif stage == 7:
            landed(d_w.at[c, y, other], SECOND)
            mine = d_w.at[c, y]
            for k in (2, 1, 3):
                send(mine, mine, *sems(LAST), y_peers[k - 1])
            left(d_w.at[c, y, x], SECOND)
        else:
            landed(d_w.at[c, pl.ds(0, NY - 1)], LAST)
            for yy in range(NY):
                for zz in range(NZ):
                    for m in range(2):
                        d_stage[c, m, :, lanes(yy * NZ + zz)] = d_w[c, yy, m, zz]
            d_store(c).start()
            left(d_w.at[c, pl.ds(0, NY - 1)], LAST)

    for k in range(1, NY):
        send(cnt.at[0], cnt.at[k], c_ss.at[0], c_rs.at[0], y_peers[k - 1])
    send(cnt.at[0], cnt.at[NY], c_ss.at[0], c_rs.at[0], partner)
    for c in range(AHEAD):
        send_raw(c)
    send(mom_t.at[other], mbuf.at[half], m_ss.at[0], m_rs.at[0], partner)
    send(swa_t.at[other], sbuf.at[half], m_ss.at[0], m_rs.at[1], partner)
    drain(cnt.at[pl.ds(0, NY)], c_rs.at[0])
    drain(cnt.at[pl.ds(0, NY)], c_ss.at[0])
    cnt_z[0] = cnt[0] + cnt[1] + cnt[2] + cnt[3]
    for k in range(1, NZ):
        send(cnt_z.at[0], cnt_z.at[k], c_ss.at[1], c_rs.at[1], z_peers[k - 1])
    for load in loads:
        load.wait()

    def slot(t, carry):
        @pl.when(t == 2)
        def _():
            drain(cnt_z.at[pl.ds(0, NZ - 1)], c_rs.at[1])
            drain(cnt_z.at[pl.ds(0, NZ - 1)], c_ss.at[1])
            acc = cnt_z[0]
            for k in range(1, NZ):
                acc += cnt_z[k]
            cnt_x[0] = acc
            send(cnt_x.at[0], cnt_x.at[1], c_ss.at[2], c_rs.at[2], partner)

        @pl.when(t == 4)
        def _():
            drain(cnt_x.at[0], c_rs.at[2])
            drain(cnt_x.at[0], c_ss.at[2])
            total[...] = (cnt_x[0] + cnt_x[1]).astype(f32)
            drain(mbuf.at[other_half], m_rs.at[0])
            drain(sbuf.at[other_half], m_rs.at[1])
            drain(mbuf, m_ss.at[0])
            for load in late_loads:
                load.wait()
            mfull[...] = mbuf[...].T
            sfull[...] = sbuf[...].T

        for kind, stage in ORDER:
            first, count, fn = (A_AT, na, a_stage_fn) if kind == "A" else (D_AT, nd, d_stage_fn)
            c = t - first[stage]
            pl.when((c >= 0) & (c < count))(functools.partial(fn, stage, c))
        send_raw(t + AHEAD)

        @pl.when(t == max(na + A_AT[5], nd + D_AT[5]))
        def _():
            mbuf[...] = mfull[...].T
            sbuf[...] = sfull[...].T
            send(mbuf.at[other_half], nmom_t.at[x], m_ss.at[0], m_rs.at[0], partner)
            send(sbuf.at[other_half], nswa_t.at[x], m_ss.at[0], m_rs.at[1], partner)
            pltpu.make_async_copy(mbuf.at[half], nmom_t.at[x], l_sem.at[5]).start()
            pltpu.make_async_copy(sbuf.at[half], nswa_t.at[x], l_sem.at[6]).start()

        return carry

    lax.fori_loop(0, max(na + A_AT[-1], nd + D_AT[-1]), slot, 0)
    pltpu.make_async_copy(mbuf.at[half], nmom_t.at[x], l_sem.at[5]).wait()
    pltpu.make_async_copy(sbuf.at[half], nswa_t.at[x], l_sem.at[6]).wait()
    drain(nmom_t.at[other], m_rs.at[0])
    drain(nswa_t.at[other], m_rs.at[1])
    drain(mbuf, m_ss.at[0])

    def wait_out(c, carry):
        @pl.when(c < na)
        def _():
            a_store(c, x).wait()
            a_store(c, other).wait()

        @pl.when(c < nd)
        def _():
            d_store(c).wait()

        return carry

    lax.fori_loop(0, max(na, nd), wait_out, 0)


def per_device(local, outer, momentum, swa, tokens, step_no):
    mats, rows, width = outer.shape
    na = rows // R // 2
    nd = rows // R - na
    f32, bf16, i32 = jnp.float32, jnp.bfloat16, jnp.int32
    vmem, dma = pltpu.VMEM, pltpu.SemaphoreType.DMA
    wide = NZ * LANES
    scratch = [
        vmem((na, NY - 1, mats, R, wide), bf16),
        vmem((mats, na * R, wide), bf16),
        vmem((mats, na * R, wide), bf16),
        vmem((na, NZ, mats, R, LANES), f32),
        vmem((na, 4, 2, mats, R, LANES), f32),
        vmem((na, mats, R, LANES), f32),
        vmem((na, R, LANES), f32),
        vmem((na, NY, NZ, R, LANES), bf16),
        vmem((na, NY, NZ, R, LANES), bf16),
        vmem((na, mats, R, width), bf16),
        vmem((nd, R, width), bf16),
        vmem((nd * R, width), bf16),
        vmem((nd * R, width), bf16),
        vmem((nd, NZ, NY, R, LANES), f32),
        vmem((nd, 4, 2, NY, R, LANES), f32),
        vmem((nd, NY, R, LANES), f32),
        vmem((nd, NY - 1, R, LANES), f32),
        vmem((nd, NY, NX, NZ, R, LANES), bf16),
        vmem((nd, mats, R, width), bf16),
        vmem((NY + 1, 8, LANES), i32),
        vmem((NZ, 8, LANES), i32),
        vmem((2, 8, LANES), i32),
        vmem((8, LANES), f32),
        vmem((LANES, rows), f32),
        vmem((LANES, rows), f32),
        vmem((rows, LANES), f32),
        vmem((rows, LANES), f32),
        vmem((rows, LANES), bf16),
        dma((2, 9)), dma((na, 9)), dma((2, 9)), dma((nd, 9)), dma((2, 4)),
        dma((3,)), dma((3,)), dma((1,)), dma((2,)), dma((7,)), dma((na + nd, 2)),
    ]
    anywhere = pl.BlockSpec(memory_space=pl.ANY)
    in_hbm = pl.BlockSpec(memory_space=pltpu.HBM)
    in_smem = pl.BlockSpec(memory_space=pltpu.SMEM)
    turned = jax.ShapeDtypeStruct((mats, LANES // 2, rows), f32)
    shapes = (jax.ShapeDtypeStruct(outer.shape, bf16), turned, turned)
    results = pl.pallas_call(
        functools.partial(kernel, na, nd, rows),
        out_shape=shapes,
        in_specs=[in_hbm] * 4 + [in_smem] * 2,
        out_specs=(anywhere,) * 3,
        scratch_shapes=scratch,
        compiler_params=pltpu.CompilerParams(
            collective_id=0, has_side_effects=True, vmem_limit_bytes=47 * 2**20
        ),
    )(local, outer, jnp.swapaxes(momentum, 1, 2), jnp.swapaxes(swa, 1, 2), tokens, step_no)
    new_weights, new_mom, new_swa = results
    return new_weights, jnp.swapaxes(new_mom, 1, 2), jnp.swapaxes(new_swa, 1, 2)


def solution(mesh):
    return jax.shard_map(
        per_device,
        mesh=mesh,
        in_specs=(
            P("rep", None, "fsdp", None),
            P(None, "fsdp", None),
            P(None, "fsdp", "rep"),
            P(None, "fsdp", "rep"),
            P("rep"),
            P(),
        ),
        out_specs=(P(None, "fsdp", None), P(None, "fsdp", "rep"), P(None, "fsdp", "rep")),
        check_vma=False,
    )
```

```python
import functools

import jax
import jax.numpy as jnp
from jax import lax
from jax.experimental import pallas as pl
from jax.experimental.pallas import tpu as pltpu
from jax.sharding import PartitionSpec as P

MESH = pl.DeviceIdType.MESH
NY, NZ, NX = 4, 8, 2
LANES = 128
R = 16
AHEAD = 3
NB = 5
ND = 7
A_AT = (0, 1, 2, 3, 4, 5, 6, 8, 10)
B_AT = (0, 1, 2, 3, 4, 5, 6, 8, 10, 12, 13, 14)
D_AT = (0, 1, 2, 3, 4, 6, 7, 9, 10, 12)
ORDER = (
    ("B", 9), ("A", 0), ("A", 1), ("D", 0), ("A", 2), ("A", 3), ("A", 7), ("D", 7), ("A", 4), ("A", 5), ("D", 5), ("B", 8), ("B", 10), ("D", 9), ("A", 6), ("D", 1), ("B", 11), ("B", 5), ("B", 7), ("B", 6), ("A", 8), ("D", 2), ("D", 8), ("D", 6), ("D", 3), ("D", 4),
)
FLIGHT = 1 + max(b - a for at in (A_AT, B_AT, D_AT) for a, b in zip(at, at[1:]))
RAW, RING, MID, FIRST, SECOND, LAST = 0, 1, 5, 6, 7, 8


def kernel(
    na, nd, rows,
    local, outer, mom_t, tokens,
    out, grad_t, upd_t,
    a_raw, a_own, a_out, a_p, a_r, a_q, a_qx, a_w, a_wx, b_w, a_stage,
    d_raw, d_own, d_out, d_p, d_r, d_q, d_qy, d_w, d_stage,
    cnt, cnt_z, cnt_x, total, gbuf, ubuf, mfull, gfull, ufull, ofull,
    a_ss, a_rs, d_ss, d_rs, raw_ss, c_ss, c_rs, m_ss, m_rs, l_sem, o_sem,
):
    f32, bf16 = jnp.float32, jnp.bfloat16
    rep, fsdp = lax.axis_index("rep"), lax.axis_index("fsdp")
    y, z, x = rep // (NZ * NX), (rep // NX) % NZ, rep % NX
    other = 1 - x
    d_row = na * R

    def at(yy, zz, xx):
        return ((lax.rem(yy + 2 * NY, NY) * NZ + lax.rem(zz + 2 * NZ, NZ)) * NX + xx, fsdp)

    def zi(k):
        return lax.rem(z + k + 2 * NZ, NZ)

    def yi(k):
        return lax.rem(y + k + 2 * NY, NY)

    def send(src, dst, ss, rs, where):
        pltpu.make_async_remote_copy(
            src_ref=src, dst_ref=dst, send_sem=ss, recv_sem=rs, device_id=where, device_id_type=MESH
        ).start()

    def drain(ref, sem):
        pltpu.make_async_copy(ref, ref, sem).wait()

    partner = at(y, z, other)
    y_peers = [at(y + k, z, x) for k in range(1, NY)]
    z_peers = [at(y, z + k, x) for k in range(1, NZ)]

    def a_rows(c):
        return pl.ds(pl.multiple_of(c * R, R), R)

    def d_rows(c):
        return pl.ds(pl.multiple_of(d_row + c * R, R), R)

    def lanes(block):
        return pl.ds(block * LANES, LANES)

    def cnt_f(k):
        return cnt[k, 0:1, :].astype(f32)

    half = pl.ds(pl.multiple_of(x * (LANES // 2), LANES // 2), LANES // 2)
    other_half = pl.ds(pl.multiple_of(other * (LANES // 2), LANES // 2), LANES // 2)
    ycols = pl.ds(pl.multiple_of(y * (NZ * LANES), NZ * LANES), NZ * LANES)
    cols = pl.ds(pl.multiple_of((y * NZ + z) * LANES, LANES), LANES)
    arows, drows = pl.ds(0, na * R), pl.ds(d_row, nd * R)
    loads = [
        pltpu.make_async_copy(local.at[0, :, arows, ycols], a_own, l_sem.at[1]),
        pltpu.make_async_copy(outer.at[:, arows, ycols], a_out, l_sem.at[2]),
        pltpu.make_async_copy(local.at[0, x, drows, :], d_own, l_sem.at[3]),
        pltpu.make_async_copy(outer.at[x, drows, :], d_out, l_sem.at[4]),
    ]
    late_loads = [
        pltpu.make_async_copy(outer.at[x, :, cols], ofull, l_sem.at[0]),
        pltpu.make_async_copy(mom_t.at[x], gbuf.at[half], l_sem.at[5]),
    ]
    for load in loads + late_loads:
        load.start()
    cnt[0] = jnp.full((8, LANES), tokens[0], jnp.int32)

    barrier = pltpu.get_barrier_semaphore()
    peers = y_peers + z_peers + [partner]
    for peer in peers:
        pl.semaphore_signal(barrier, inc=1, device_id=peer, device_id_type=MESH)
    pl.semaphore_wait(barrier, len(peers))

    def send_raw(c):
        @pl.when(c < na)
        def _():
            for k in (2, 1, 3):
                theirs = pl.ds(pl.multiple_of(yi(k) * (NZ * LANES), NZ * LANES), NZ * LANES)
                send(
                    local.at[0, :, a_rows(c), theirs], a_raw.at[c, k - 1],
                    raw_ss.at[0, c % 4], a_rs.at[c, RAW], y_peers[k - 1],
                )

        @pl.when(c < nd)
        def _():
            send(local.at[0, other, d_rows(c), :], d_raw.at[c], raw_ss.at[1, c % 4], d_rs.at[c, RAW], partner)

    def ring_stage(stage, c, sign, p, r, ss, rs):
        up, down = at(y, z + sign, x), at(y, z - sign, x)

        def step(k, long, short):
            send(long, r.at[c, k, 0], ss.at[c % FLIGHT, RING + k], rs.at[c, RING + k], up)
            if k < 3:
                send(short, r.at[c, k, 1], ss.at[c % FLIGHT, RING + k], rs.at[c, RING + k], down)

        if stage == 0:
            step(0, p.at[c, zi(4 * sign)], p.at[c, zi(-3 * sign)])
            return
        k = stage - 1
        came = r.at[c, k] if k < 3 else r.at[c, k, 0]
        drain(came, rs.at[c, RING + k])
        if k < 3:
            r[c, k, 0] += p[c, zi((3 - k) * sign)]
            if k < 2:
                r[c, k, 1] += p[c, zi(-(2 - k) * sign)]
            step(k + 1, r.at[c, k, 0], r.at[c, k, 1])
        drain(came, ss.at[c % FLIGHT, RING + k])

    def update(rws, pg_sum):
        o = ofull[rws, :].astype(f32)
        pg = pg_sum / total[0:1, :]
        upd = o - 0.7 * (pg + 0.9 * (0.9 * mfull[rws, :] + pg))
        gfull[rws, :] = pg
        ufull[rws, :] = upd
        return upd.astype(bf16)

    def a_store(c, m):
        return pltpu.make_async_copy(a_stage.at[c, m], out.at[m, a_rows(c), :], o_sem.at[c, m])

    def a_stage_fn(stage, c):
        ring = functools.partial(ring_stage, c=c, sign=1 - 2 * (c % 2), p=a_p, r=a_r, ss=a_ss, rs=a_rs)

        def sems(k):
            return a_ss.at[c % FLIGHT, k], a_rs.at[c, k]

        def landed(ref, k):
            drain(ref, a_rs.at[c, k])

        def left(ref, k):
            drain(ref, a_ss.at[c % FLIGHT, k])

        if stage == 0:
            landed(a_raw.at[c], RAW)
            for zz in range(NZ):
                for m in range(2):
                    o = a_out[m, a_rows(c), lanes(zz)].astype(f32)
                    acc = cnt_f(0) * (o - a_own[m, a_rows(c), lanes(zz)].astype(f32))
                    for k in range(1, NY):
                        acc += cnt_f(k) * (o - a_raw[c, k - 1, m, :, lanes(zz)].astype(f32))
                    a_p[c, zz, m] = acc
            ring(0)
            drain(a_raw.at[c], raw_ss.at[0, c % 4])
        elif stage <= 3:
            ring(stage)
        elif stage == 4:
            ring(4)
            a_q[c] = a_p[c, z] + a_r[c, 3, 0] + a_r[c, 2, 1]
            send(a_q.at[c, other], a_qx.at[c], *sems(MID), partner)
        elif stage == 5:
            landed(a_qx.at[c], MID)
            mine = a_w.at[c, y, z]
            mine[...] = update(a_rows(c), a_q[c, x] + a_qx[c])
            for k in (4, 3, 5, 2, 6, 1, 7):
                send(mine, mine, *sems(FIRST), z_peers[k - 1])
            left(a_qx.at[c], MID)
        elif stage == 6:
            landed(a_w.at[c, y, pl.ds(0, NZ - 1)], FIRST)
            mine = a_w.at[c, y]
            for k in (2, 1, 3):
                send(mine, mine, *sems(SECOND), y_peers[k - 1])
            left(a_w.at[c, y, pl.ds(0, NZ - 1)], FIRST)
        elif stage == 7:
            landed(a_w.at[c, pl.ds(0, NY - 1)], SECOND)
            send(a_w.at[c], a_wx.at[c], *sems(LAST), partner)
            for yy in range(NY):
                for zz in range(NZ):
                    a_stage[c, x, :, lanes(yy * NZ + zz)] = a_w[c, yy, zz]
            a_store(c, x).start()
            left(a_w.at[c, pl.ds(0, NY - 1)], SECOND)
        else:
            landed(a_wx.at[c], LAST)
            for yy in range(NY):
                for zz in range(NZ):
                    a_stage[c, other, :, lanes(yy * NZ + zz)] = a_wx[c, yy, zz]
            a_store(c, other).start()
            left(a_wx.at[c], LAST)

    def b_stage_fn(stage, c):
        sign = 1 - 2 * (c % 2)
        up, down = at(y, z + sign, x), at(y, z - sign, x)

        def sems(k):
            return a_ss.at[c % FLIGHT, k], a_rs.at[c, k]

        def landed(ref, k):
            drain(ref, a_rs.at[c, k])

        def left(ref, k):
            drain(ref, a_ss.at[c % FLIGHT, k])

        def step(k):
            long, short = b_w.at[c, zi(-k * sign)], b_w.at[c, zi(k * sign)]
            send(long, long, *sems(LAST + k), up)
            if k < 3:
                send(short, short, *sems(LAST + k), down)

        if stage == 5:
            landed(a_qx.at[c], MID)
            mine = b_w.at[c, z, y, x]
            mine[...] = update(a_rows(c), a_q[c, x] + a_qx[c])
            send(mine, mine, *sems(FIRST), partner)
            left(a_qx.at[c], MID)
        elif stage == 6:
            landed(b_w.at[c, z, y, other], FIRST)
            mine = b_w.at[c, z, y]
            for k in (2, 1, 3):
                send(mine, mine, *sems(SECOND), y_peers[k - 1])
            left(b_w.at[c, z, y, other], FIRST)
        elif stage == 7:
            landed(b_w.at[c, z, pl.ds(0, NY - 1)], SECOND)
            step(0)
            left(b_w.at[c, z, pl.ds(0, NY - 1)], SECOND)
        else:
            k = stage - 8
            came = b_w.at[c, pl.ds(0, 2 if k < 3 else 1)]
            landed(came, LAST + k)
            if k < 3:
                step(k + 1)
            else:
                for yy in range(NY):
                    for zz in range(NZ):
                        for m in range(2):
                            a_stage[c, m, :, lanes(yy * NZ + zz)] = b_w[c, zz, yy, m]
                for m in range(2):
                    a_store(c, m).start()
            left(came, LAST + k)

    def d_store(c):
        return pltpu.make_async_copy(d_stage.at[c], out.at[:, d_rows(c), :], o_sem.at[na + c, 0])

    def d_stage_fn(stage, c):
        ring = functools.partial(ring_stage, c=c, sign=2 * (c % 2) - 1, p=d_p, r=d_r, ss=d_ss, rs=d_rs)

        def sems(k):
            return d_ss.at[c % FLIGHT, k], d_rs.at[c, k]

        def landed(ref, k):
            drain(ref, d_rs.at[c, k])

        def left(ref, k):
            drain(ref, d_ss.at[c % FLIGHT, k])

        if stage == 0:
            landed(d_raw.at[c], RAW)
            own = pl.ds(pl.multiple_of(c * R, R), R)
            for yy in range(NY):
                for zz in range(NZ):
                    sl = lanes(yy * NZ + zz)
                    o = d_out[own, sl].astype(f32)
                    mine = cnt_f(0) * (o - d_own[own, sl].astype(f32))
                    d_p[c, zz, yy] = mine + cnt_f(NY) * (o - d_raw[c, :, sl].astype(f32))
            ring(0)
            drain(d_raw.at[c], raw_ss.at[1, c % 4])
        elif stage <= 3:
            ring(stage)
        elif stage == 4:
            ring(4)
            d_q[c] = d_p[c, z] + d_r[c, 3, 0] + d_r[c, 2, 1]
            for k in (2, 1, 3):
                send(d_q.at[c, yi(k)], d_qy.at[c, k - 1], *sems(MID), y_peers[k - 1])
        elif stage == 5:
            landed(d_qy.at[c], MID)
            mine = d_w.at[c, y, x, z]
            mine[...] = update(d_rows(c), d_q[c, y] + d_qy[c, 0] + d_qy[c, 1] + d_qy[c, 2])
            for k in (4, 3, 5, 2, 6, 1, 7):
                send(mine, mine, *sems(FIRST), z_peers[k - 1])
            left(d_qy.at[c], MID)
        elif stage == 6:
            landed(d_w.at[c, y, x, pl.ds(0, NZ - 1)], FIRST)
            mine = d_w.at[c, y, x]
            send(mine, mine, *sems(SECOND), partner)
            left(d_w.at[c, y, x, pl.ds(0, NZ - 1)], FIRST)
        elif stage == 7:
            landed(d_w.at[c, y, other], SECOND)
            mine = d_w.at[c, y]
            for k in (1, 3):
                send(mine, mine, *sems(LAST), y_peers[k - 1])
            left(d_w.at[c, y, x], SECOND)
        elif stage == 8:
            landed(d_w.at[c, pl.ds(0, 2)], LAST)
            for k, m in ((1, 0), (-1, 1)):
                theirs = d_w.at[c, yi(-k), m]
                send(theirs, theirs, *sems(LAST + 1), at(y + k, z, x))
            left(d_w.at[c, pl.ds(0, 2)], LAST)
        else:
            landed(d_w.at[c, 0], LAST + 1)
            for yy in range(NY):
                for zz in range(NZ):
                    for m in range(2):
                        d_stage[c, m, :, lanes(yy * NZ + zz)] = d_w[c, yy, m, zz]
            d_store(c).start()
            left(d_w.at[c, 0], LAST + 1)

    for k in range(1, NY):
        send(cnt.at[0], cnt.at[k], c_ss.at[0], c_rs.at[0], y_peers[k - 1])
    send(cnt.at[0], cnt.at[NY], c_ss.at[0], c_rs.at[0], partner)
    for c in range(AHEAD):
        send_raw(c)
    send(mom_t.at[other], gbuf.at[half], m_ss.at[0], m_rs.at[0], partner)
    drain(cnt.at[pl.ds(0, NY)], c_rs.at[0])
    drain(cnt.at[pl.ds(0, NY)], c_ss.at[0])
    cnt_z[0] = cnt[0] + cnt[1] + cnt[2] + cnt[3]
    for k in range(1, NZ):
        send(cnt_z.at[0], cnt_z.at[k], c_ss.at[1], c_rs.at[1], z_peers[k - 1])
    for load in loads:
        load.wait()

    def slot(t, carry):
        @pl.when(t == 2)
        def _():
            drain(cnt_z.at[pl.ds(0, NZ - 1)], c_rs.at[1])
            drain(cnt_z.at[pl.ds(0, NZ - 1)], c_ss.at[1])
            acc = cnt_z[0]
            for k in range(1, NZ):
                acc += cnt_z[k]
            cnt_x[0] = acc
            send(cnt_x.at[0], cnt_x.at[1], c_ss.at[2], c_rs.at[2], partner)

        @pl.when(t == 4)
        def _():
            drain(cnt_x.at[0], c_rs.at[2])
            drain(cnt_x.at[0], c_ss.at[2])
            total[...] = (cnt_x[0] + cnt_x[1]).astype(f32)
            drain(gbuf.at[other_half], m_rs.at[0])
            drain(gbuf.at[other_half], m_ss.at[0])
            for load in late_loads:
                load.wait()
            mfull[...] = gbuf[...].T

        for kind, stage in ORDER:
            if kind == "D":
                c, low, high, fn = t - D_AT[stage], 0, nd, d_stage_fn
            elif kind == "B":
                c, low, high, fn = t - B_AT[stage], 0, NB, b_stage_fn
            else:
                c, low, high, fn = t - A_AT[stage], NB if stage > 4 else 0, na, a_stage_fn
            pl.when((c >= low) & (c < high))(functools.partial(fn, stage, c))
        send_raw(t + AHEAD)

        @pl.when(t == max(na + A_AT[5], NB + B_AT[5], nd + D_AT[5]))
        def _():
            gbuf[...] = gfull[...].T
            ubuf[...] = ufull[...].T
            send(gbuf.at[other_half], grad_t.at[x], m_ss.at[0], m_rs.at[0], partner)
            send(ubuf.at[other_half], upd_t.at[x], m_ss.at[1], m_rs.at[1], partner)
            pltpu.make_async_copy(gbuf.at[half], grad_t.at[x], l_sem.at[5]).start()
            pltpu.make_async_copy(ubuf.at[half], upd_t.at[x], l_sem.at[6]).start()

        return carry

    lax.fori_loop(0, max(na + A_AT[-1], NB + B_AT[-1], nd + D_AT[-1]), slot, 0)
    pltpu.make_async_copy(gbuf.at[half], grad_t.at[x], l_sem.at[5]).wait()
    pltpu.make_async_copy(ubuf.at[half], upd_t.at[x], l_sem.at[6]).wait()
    drain(grad_t.at[other], m_rs.at[0])
    drain(upd_t.at[other], m_rs.at[1])
    drain(gbuf.at[other_half], m_ss.at[0])
    drain(ubuf.at[other_half], m_ss.at[1])

    def wait_out(c, carry):
        @pl.when(c < na)
        def _():
            a_store(c, x).wait()
            a_store(c, other).wait()

        @pl.when(c < nd)
        def _():
            d_store(c).wait()

        return carry

    lax.fori_loop(0, max(na, nd), wait_out, 0)


def per_device(local, outer, momentum, swa, tokens, step_no):
    mats, rows, width = outer.shape
    nd = ND
    na = rows // R - nd
    f32, bf16, i32 = jnp.float32, jnp.bfloat16, jnp.int32
    vmem, dma = pltpu.VMEM, pltpu.SemaphoreType.DMA
    wide = NZ * LANES
    scratch = [
        vmem((na, NY - 1, mats, R, wide), bf16),
        vmem((mats, na * R, wide), bf16),
        vmem((mats, na * R, wide), bf16),
        vmem((na, NZ, mats, R, LANES), f32),
        vmem((na, 4, 2, mats, R, LANES), f32),
        vmem((na, mats, R, LANES), f32),
        vmem((na, R, LANES), f32),
        vmem((na, NY, NZ, R, LANES), bf16),
        vmem((na, NY, NZ, R, LANES), bf16),
        vmem((NB, NZ, NY, NX, R, LANES), bf16),
        vmem((na, mats, R, width), bf16),
        vmem((nd, R, width), bf16),
        vmem((nd * R, width), bf16),
        vmem((nd * R, width), bf16),
        vmem((nd, NZ, NY, R, LANES), f32),
        vmem((nd, 4, 2, NY, R, LANES), f32),
        vmem((nd, NY, R, LANES), f32),
        vmem((nd, NY - 1, R, LANES), f32),
        vmem((nd, NY, NX, NZ, R, LANES), bf16),
        vmem((nd, mats, R, width), bf16),
        vmem((NY + 1, 8, LANES), i32),
        vmem((NZ, 8, LANES), i32),
        vmem((2, 8, LANES), i32),
        vmem((8, LANES), f32),
        vmem((LANES, rows), f32),
        vmem((LANES, rows), f32),
        vmem((rows, LANES), f32),
        vmem((rows, LANES), f32),
        vmem((rows, LANES), f32),
        vmem((rows, LANES), bf16),
        dma((FLIGHT, 12)), dma((na, 12)), dma((FLIGHT, 10)), dma((nd, 10)), dma((2, 4)),
        dma((3,)), dma((3,)), dma((2,)), dma((2,)), dma((7,)), dma((na + nd, 2)),
    ]
    anywhere = pl.BlockSpec(memory_space=pl.ANY)
    in_hbm = pl.BlockSpec(memory_space=pltpu.HBM)
    in_smem = pl.BlockSpec(memory_space=pltpu.SMEM)
    turned = jax.ShapeDtypeStruct((mats, LANES // 2, rows), f32)
    shapes = (jax.ShapeDtypeStruct(outer.shape, bf16), turned, turned)
    results = pl.pallas_call(
        functools.partial(kernel, na, nd, rows),
        out_shape=shapes,
        in_specs=[in_hbm] * 3 + [in_smem],
        out_specs=(anywhere,) * 3,
        scratch_shapes=scratch,
        compiler_params=pltpu.CompilerParams(
            collective_id=0, has_side_effects=True, vmem_limit_bytes=47 * 2**20
        ),
    )(local, outer, jnp.swapaxes(momentum, 1, 2), tokens)
    new_weights, grad, updated = results
    grad, updated = jnp.swapaxes(grad, 1, 2), jnp.swapaxes(updated, 1, 2)
    divisor = step_no[0].astype(f32) + 1.0
    return new_weights, 0.9 * momentum + grad, swa + (updated - swa) / divisor


def solution(mesh):
    return jax.shard_map(
        per_device,
        mesh=mesh,
        in_specs=(
            P("rep", None, "fsdp", None),
            P(None, "fsdp", None),
            P(None, "fsdp", "rep"),
            P(None, "fsdp", "rep"),
            P("rep"),
            P(),
        ),
        out_specs=(P(None, "fsdp", None), P(None, "fsdp", "rep"), P(None, "fsdp", "rep")),
        check_vma=False,
    )
```

```python
import functools

import jax
import jax.numpy as jnp
from jax import lax
from jax.experimental import pallas as pl
from jax.experimental.pallas import tpu as pltpu
from jax.sharding import PartitionSpec as P

MESH = pl.DeviceIdType.MESH
NY, NZ, NX = 4, 8, 2
LANES = 128
R = 16
AHEAD = 3
NB = 5
ND = 7
A_AT = (0, 1, 2, 3, 4, 5, 6, 8)
B_AT = (0, 1, 2, 3, 4, 5, 6, 8, 10, 12, 13, 14)
D_AT = (0, 1, 2, 3, 4, 6, 7, 9, 10)
ORDER = (
    ("B", 9), ("A", 0), ("A", 1), ("D", 0), ("A", 2), ("A", 3), ("A", 7), ("D", 7), ("A", 4), ("A", 5), ("D", 5), ("B", 8), ("B", 10), ("A", 6), ("D", 1), ("B", 11), ("B", 5), ("B", 7), ("B", 6), ("D", 2), ("D", 8), ("D", 6), ("D", 3), ("D", 4),
)
RAW, RING, MID, FIRST, SECOND, LAST = 0, 1, 5, 6, 7, 8


def kernel(
    na, nd, rows,
    local, outer, mom_t, tokens,
    out, grad_t, upd_t,
    a_raw, a_own, a_out, a_p, a_r, a_q, a_qx, a_v, b_w, b_stage,
    d_raw, d_own, d_out, d_p, d_r, d_q, d_qy, d_v,
    cnt, cnt_z, cnt_x, total, gbuf, ubuf, mfull, gfull, ufull, ofull,
    a_ss, b_ss, a_rs, d_ss, d_rs, c_ss, c_rs, m_ss, m_rs, l_sem, o_sem, v_sem, end_s,
):
    f32, bf16 = jnp.float32, jnp.bfloat16
    rep, fsdp = lax.axis_index("rep"), lax.axis_index("fsdp")
    y, z, x = rep // (NZ * NX), (rep // NX) % NZ, rep % NX
    other = 1 - x
    d_row = na * R

    def at(yy, zz, xx):
        return ((lax.rem(yy + 2 * NY, NY) * NZ + lax.rem(zz + 2 * NZ, NZ)) * NX + xx, fsdp)

    def zi(k):
        return lax.rem(z + k + 2 * NZ, NZ)

    def yi(k):
        return lax.rem(y + k + 2 * NY, NY)

    def send(src, dst, ss, rs, where):
        pltpu.make_async_remote_copy(
            src_ref=src, dst_ref=dst, send_sem=ss, recv_sem=rs, device_id=where, device_id_type=MESH
        ).start()

    def drain(ref, sem):
        pltpu.make_async_copy(ref, ref, sem).wait()

    partner = at(y, z, other)
    y_peers = [at(y + k, z, x) for k in range(1, NY)]
    z_peers = [at(y, z + k, x) for k in range(1, NZ)]

    def a_rows(c):
        return pl.ds(pl.multiple_of(c * R, R), R)

    def d_rows(c):
        return pl.ds(pl.multiple_of(d_row + c * R, R), R)

    def lanes(block):
        return pl.ds(block * LANES, LANES)

    def cnt_f(k):
        return cnt[k, 0:1, :].astype(f32)

    half = pl.ds(pl.multiple_of(x * (LANES // 2), LANES // 2), LANES // 2)
    other_half = pl.ds(pl.multiple_of(other * (LANES // 2), LANES // 2), LANES // 2)
    ycols = pl.ds(pl.multiple_of(y * (NZ * LANES), NZ * LANES), NZ * LANES)
    cols = pl.ds(pl.multiple_of((y * NZ + z) * LANES, LANES), LANES)
    arows, drows = pl.ds(0, na * R), pl.ds(d_row, nd * R)
    loads = [
        pltpu.make_async_copy(local.at[0, :, arows, ycols], a_own, l_sem.at[1]),
        pltpu.make_async_copy(outer.at[:, arows, ycols], a_out, l_sem.at[2]),
        pltpu.make_async_copy(local.at[0, x, drows, :], d_own, l_sem.at[3]),
        pltpu.make_async_copy(outer.at[x, drows, :], d_out, l_sem.at[4]),
    ]
    late_loads = [
        pltpu.make_async_copy(outer.at[x, :, cols], ofull, l_sem.at[0]),
        pltpu.make_async_copy(mom_t.at[x], gbuf.at[half], l_sem.at[5]),
    ]
    for load in loads + late_loads:
        load.start()
    cnt[0] = jnp.full((8, LANES), tokens[0], jnp.int32)

    barrier = pltpu.get_barrier_semaphore()
    peers = y_peers + z_peers + [partner]
    for peer in peers:
        pl.semaphore_signal(barrier, inc=1, device_id=peer, device_id_type=MESH)
    pl.semaphore_wait(barrier, len(peers))

    def send_raw(c):
        @pl.when(c < na)
        def _():
            for k in (2, 1, 3):
                theirs = pl.ds(pl.multiple_of(yi(k) * (NZ * LANES), NZ * LANES), NZ * LANES)
                send(
                    local.at[0, :, a_rows(c), theirs], a_raw.at[c, k - 1],
                    a_ss.at[RAW], a_rs.at[c, RAW], y_peers[k - 1],
                )

        @pl.when(c < nd)
        def _():
            send(local.at[0, other, d_rows(c), :], d_raw.at[c], d_ss.at[RAW], d_rs.at[c, RAW], partner)

    def ring_stage(stage, c, sign, p, r, ss, rs):
        up, down = at(y, z + sign, x), at(y, z - sign, x)

        def step(k, long, short):
            send(long, r.at[c, k, 0], ss.at[RING + k], rs.at[c, RING + k], up)
            if k < 3:
                send(short, r.at[c, k, 1], ss.at[RING + k], rs.at[c, RING + k], down)

        if stage == 0:
            step(0, p.at[c, zi(4 * sign)], p.at[c, zi(-3 * sign)])
            return
        k = stage - 1
        came = r.at[c, k] if k < 3 else r.at[c, k, 0]
        drain(came, rs.at[c, RING + k])
        if k < 3:
            r[c, k, 0] += p[c, zi((3 - k) * sign)]
            if k < 2:
                r[c, k, 1] += p[c, zi(-(2 - k) * sign)]
            step(k + 1, r.at[c, k, 0], r.at[c, k, 1])

    def update(rws, pg_sum):
        o = ofull[rws, :].astype(f32)
        pg = pg_sum / total[0:1, :]
        upd = o - 0.7 * (pg + 0.9 * (0.9 * mfull[rws, :] + pg))
        gfull[rws, :] = pg
        ufull[rws, :] = upd
        return upd.astype(bf16)

    def a_stage_fn(stage, c):
        ring = functools.partial(ring_stage, c=c, sign=1 - 2 * (c % 2), p=a_p, r=a_r, ss=a_ss, rs=a_rs)

        def sems(k):
            return a_ss.at[k], a_rs.at[c, k]

        def landed(ref, k):
            drain(ref, a_rs.at[c, k])

        if stage == 0:
            landed(a_raw.at[c], RAW)
            for zz in range(NZ):
                for m in range(2):
                    o = a_out[m, a_rows(c), lanes(zz)].astype(f32)
                    acc = cnt_f(0) * (o - a_own[m, a_rows(c), lanes(zz)].astype(f32))
                    for k in range(1, NY):
                        acc += cnt_f(k) * (o - a_raw[c, k - 1, m, :, lanes(zz)].astype(f32))
                    a_p[c, zz, m] = acc
            ring(0)
        elif stage <= 3:
            ring(stage)
        elif stage == 4:
            ring(4)
            a_q[c] = a_p[c, z] + a_r[c, 3, 0] + a_r[c, 2, 1]
            send(a_q.at[c, other], a_qx.at[c], *sems(MID), partner)
        elif stage == 5:
            landed(a_qx.at[c], MID)
            a_v[c] = update(a_rows(c), a_q[c, x] + a_qx[c])
            place = out.at[x, a_rows(c), cols]
            pltpu.make_async_copy(a_v.at[c], place, v_sem.at[0, c % 4]).start()
            for k in (4, 3, 5, 2, 6, 1, 7):
                send(a_v.at[c], place, *sems(FIRST), z_peers[k - 1])
        elif stage == 6:
            landed(out.at[x, a_rows(c), pl.ds(0, (NZ - 1) * LANES)], FIRST)
            drain(a_v.at[c], v_sem.at[0, c % 4])
            place = out.at[x, a_rows(c), ycols]
            for k in (2, 1, 3):
                send(place, place, *sems(SECOND), y_peers[k - 1])
        else:
            landed(out.at[x, a_rows(c), pl.ds(0, (NY - 1) * NZ * LANES)], SECOND)
            place = out.at[x, a_rows(c), :]
            send(place, place, a_ss.at[LAST], end_s.at[0], partner)

    def b_stage_fn(stage, c):
        sign = 1 - 2 * (c % 2)
        up, down = at(y, z + sign, x), at(y, z - sign, x)

        def sems(k):
            return b_ss.at[k], a_rs.at[c, k]

        def landed(ref, k):
            drain(ref, a_rs.at[c, k])

        def step(k):
            long, short = b_w.at[c, zi(-k * sign)], b_w.at[c, zi(k * sign)]
            send(long, long, *sems(LAST + k), up)
            if k < 3:
                send(short, short, *sems(LAST + k), down)

        if stage == 5:
            landed(a_qx.at[c], MID)
            mine = b_w.at[c, z, y, x]
            mine[...] = update(a_rows(c), a_q[c, x] + a_qx[c])
            send(mine, mine, *sems(FIRST), partner)
        elif stage == 6:
            landed(b_w.at[c, z, y, other], FIRST)
            mine = b_w.at[c, z, y]
            for k in (2, 1, 3):
                send(mine, mine, *sems(SECOND), y_peers[k - 1])
        elif stage == 7:
            landed(b_w.at[c, z, pl.ds(0, NY - 1)], SECOND)
            step(0)
        else:
            k = stage - 8
            came = b_w.at[c, pl.ds(0, 2 if k < 3 else 1)]
            landed(came, LAST + k)
            if k < 3:
                step(k + 1)
            else:
                for yy in range(NY):
                    for zz in range(NZ):
                        for m in range(2):
                            b_stage[c, m, :, lanes(yy * NZ + zz)] = b_w[c, zz, yy, m]
                pltpu.make_async_copy(b_stage.at[c], out.at[:, a_rows(c), :], o_sem).start()

    def d_stage_fn(stage, c):
        ring = functools.partial(ring_stage, c=c, sign=2 * (c % 2) - 1, p=d_p, r=d_r, ss=d_ss, rs=d_rs)

        def sems(k):
            return d_ss.at[k], d_rs.at[c, k]

        def landed(ref, k):
            drain(ref, d_rs.at[c, k])

        if stage == 0:
            landed(d_raw.at[c], RAW)
            own = pl.ds(pl.multiple_of(c * R, R), R)
            for yy in range(NY):
                for zz in range(NZ):
                    sl = lanes(yy * NZ + zz)
                    o = d_out[own, sl].astype(f32)
                    mine = cnt_f(0) * (o - d_own[own, sl].astype(f32))
                    d_p[c, zz, yy] = mine + cnt_f(NY) * (o - d_raw[c, :, sl].astype(f32))
            ring(0)
        elif stage <= 3:
            ring(stage)
        elif stage == 4:
            ring(4)
            d_q[c] = d_p[c, z] + d_r[c, 3, 0] + d_r[c, 2, 1]
            for k in (2, 1, 3):
                send(d_q.at[c, yi(k)], d_qy.at[c, k - 1], *sems(MID), y_peers[k - 1])
        elif stage == 5:
            landed(d_qy.at[c], MID)
            d_v[c] = update(d_rows(c), d_q[c, y] + d_qy[c, 0] + d_qy[c, 1] + d_qy[c, 2])
            place = out.at[x, d_rows(c), cols]
            pltpu.make_async_copy(d_v.at[c], place, v_sem.at[1, c % 4]).start()
            for k in (4, 3, 5, 2, 6, 1, 7):
                send(d_v.at[c], place, *sems(FIRST), z_peers[k - 1])
        elif stage == 6:
            landed(out.at[x, d_rows(c), pl.ds(0, (NZ - 1) * LANES)], FIRST)
            drain(d_v.at[c], v_sem.at[1, c % 4])
            place = out.at[x, d_rows(c), ycols]
            send(place, place, *sems(SECOND), partner)
        elif stage == 7:
            landed(out.at[other, d_rows(c), ycols], SECOND)
            place = out.at[:, d_rows(c), ycols]
            for k in (1, 3):
                send(place, place, *sems(LAST), y_peers[k - 1])
        else:
            landed(out.at[:, d_rows(c), pl.ds(0, 2 * NZ * LANES)], LAST)
            for k, m in ((1, 0), (-1, 1)):
                theirs = pl.ds(pl.multiple_of(yi(-k) * (NZ * LANES), NZ * LANES), NZ * LANES)
                place = out.at[m, d_rows(c), theirs]
                send(place, place, d_ss.at[LAST + 1], end_s.at[1], at(y + k, z, x))

    send_raw(0)
    for k in range(1, NY):
        send(cnt.at[0], cnt.at[k], c_ss.at[0], c_rs.at[0], y_peers[k - 1])
    send(cnt.at[0], cnt.at[NY], c_ss.at[0], c_rs.at[0], partner)
    for c in range(1, AHEAD):
        send_raw(c)
    drain(cnt.at[pl.ds(0, NY)], c_rs.at[0])
    drain(cnt.at[pl.ds(0, NY)], c_ss.at[0])
    cnt_z[0] = cnt[0] + cnt[1] + cnt[2] + cnt[3]
    for k in range(1, NZ):
        send(cnt_z.at[0], cnt_z.at[k], c_ss.at[1], c_rs.at[1], z_peers[k - 1])
    for load in loads:
        load.wait()

    def slot(t, carry):
        @pl.when(t == 2)
        def _():
            drain(cnt_z.at[pl.ds(0, NZ - 1)], c_rs.at[1])
            drain(cnt_z.at[pl.ds(0, NZ - 1)], c_ss.at[1])
            acc = cnt_z[0]
            for k in range(1, NZ):
                acc += cnt_z[k]
            cnt_x[0] = acc
            send(cnt_x.at[0], cnt_x.at[1], c_ss.at[2], c_rs.at[2], partner)
            send(mom_t.at[other], gbuf.at[half], m_ss.at[0], m_rs.at[0], partner)

        @pl.when(t == 5)
        def _():
            drain(cnt_x.at[0], c_rs.at[2])
            drain(cnt_x.at[0], c_ss.at[2])
            total[...] = (cnt_x[0] + cnt_x[1]).astype(f32)
            drain(gbuf.at[other_half], m_rs.at[0])
            drain(gbuf.at[other_half], m_ss.at[0])
            for load in late_loads:
                load.wait()
            mfull[...] = gbuf[...].T

        for kind, stage in ORDER:
            if kind == "D":
                c, low, high, fn = t - D_AT[stage], 0, nd, d_stage_fn
            elif kind == "B":
                c, low, high, fn = t - B_AT[stage], 0, NB, b_stage_fn
            else:
                c, low, high, fn = t - A_AT[stage], NB if stage > 4 else 0, na, a_stage_fn
            pl.when((c >= low) & (c < high))(functools.partial(fn, stage, c))
        send_raw(t + AHEAD)

        @pl.when(t == max(na + A_AT[5], NB + B_AT[5], nd + D_AT[5]))
        def _():
            gbuf[...] = gfull[...].T
            ubuf[...] = ufull[...].T
            send(gbuf.at[other_half], grad_t.at[x], m_ss.at[0], m_rs.at[0], partner)
            send(ubuf.at[other_half], upd_t.at[x], m_ss.at[1], m_rs.at[1], partner)
            pltpu.make_async_copy(gbuf.at[half], grad_t.at[x], l_sem.at[5]).start()
            pltpu.make_async_copy(ubuf.at[half], upd_t.at[x], l_sem.at[6]).start()

        return carry

    lax.fori_loop(0, max(na + A_AT[-1], NB + B_AT[-1], nd + D_AT[-1]), slot, 0)
    pltpu.make_async_copy(gbuf.at[half], grad_t.at[x], l_sem.at[5]).wait()
    pltpu.make_async_copy(ubuf.at[half], upd_t.at[x], l_sem.at[6]).wait()
    drain(grad_t.at[other], m_rs.at[0])
    drain(upd_t.at[other], m_rs.at[1])
    drain(gbuf.at[other_half], m_ss.at[0])
    drain(ubuf.at[other_half], m_ss.at[1])

    def part(mats, chunks, blocks):
        return out.at[pl.ds(0, mats), pl.ds(0, chunks * R), pl.ds(0, blocks * LANES)]

    for ref, sem in [
        (part(1, na - NB, NY * NZ), end_s.at[0]), (part(1, nd, 2 * NZ), end_s.at[1]), (part(2, NB, NY * NZ), o_sem),
        (a_raw, a_ss.at[RAW]), (a_r.at[:, 3, 0], a_ss.at[RING + 3]), (a_qx, a_ss.at[MID]),
        (part(1, na - NB, NZ - 1), a_ss.at[FIRST]), (part(1, na - NB, (NY - 1) * NZ), a_ss.at[SECOND]),
        (part(1, na - NB, NY * NZ), a_ss.at[LAST]),
        (b_w.at[:, 0, 0, 0], b_ss.at[FIRST]), (b_w.at[:, 0, pl.ds(0, NY - 1)], b_ss.at[SECOND]),
        (b_w.at[:, 0], b_ss.at[LAST + 3]),
        (d_raw, d_ss.at[RAW]), (d_r.at[:, 3, 0], d_ss.at[RING + 3]), (d_qy, d_ss.at[MID]),
        (part(1, nd, NZ - 1), d_ss.at[FIRST]), (part(1, nd, NZ), d_ss.at[SECOND]),
        (part(2, nd, 2 * NZ), d_ss.at[LAST]), (part(1, nd, 2 * NZ), d_ss.at[LAST + 1]),
    ]:
        drain(ref, sem)
    for k in range(3):
        drain(a_r.at[:, k], a_ss.at[RING + k])
        drain(b_w.at[:, pl.ds(0, 2)], b_ss.at[LAST + k])
        drain(d_r.at[:, k], d_ss.at[RING + k])


def per_device(local, outer, momentum, swa, tokens, step_no):
    mats, rows, width = outer.shape
    nd = ND
    na = rows // R - nd
    f32, bf16, i32 = jnp.float32, jnp.bfloat16, jnp.int32
    vmem, dma = pltpu.VMEM, pltpu.SemaphoreType.DMA
    wide = NZ * LANES
    scratch = [
        vmem((na, NY - 1, mats, R, wide), bf16),
        vmem((mats, na * R, wide), bf16),
        vmem((mats, na * R, wide), bf16),
        vmem((na, NZ, mats, R, LANES), f32),
        vmem((na, 4, 2, mats, R, LANES), f32),
        vmem((na, mats, R, LANES), f32),
        vmem((na, R, LANES), f32),
        vmem((na, R, LANES), bf16),
        vmem((NB, NZ, NY, NX, R, LANES), bf16),
        vmem((NB, mats, R, width), bf16),
        vmem((nd, R, width), bf16),
        vmem((nd * R, width), bf16),
        vmem((nd * R, width), bf16),
        vmem((nd, NZ, NY, R, LANES), f32),
        vmem((nd, 4, 2, NY, R, LANES), f32),
        vmem((nd, NY, R, LANES), f32),
        vmem((nd, NY - 1, R, LANES), f32),
        vmem((nd, R, LANES), bf16),
        vmem((NY + 1, 8, LANES), i32),
        vmem((NZ, 8, LANES), i32),
        vmem((2, 8, LANES), i32),
        vmem((8, LANES), f32),
        vmem((LANES, rows), f32),
        vmem((LANES, rows), f32),
        vmem((rows, LANES), f32),
        vmem((rows, LANES), f32),
        vmem((rows, LANES), f32),
        vmem((rows, LANES), bf16),
        dma((9,)), dma((12,)), dma((na, 12)), dma((10,)), dma((nd, 10)),
        dma((3,)), dma((3,)), dma((2,)), dma((2,)), dma((7,)), dma, dma((2, 4)), dma((2,)),
    ]
    anywhere = pl.BlockSpec(memory_space=pl.ANY)
    in_hbm = pl.BlockSpec(memory_space=pltpu.HBM)
    in_smem = pl.BlockSpec(memory_space=pltpu.SMEM)
    turned = jax.ShapeDtypeStruct((mats, LANES // 2, rows), f32)
    shapes = (jax.ShapeDtypeStruct(outer.shape, bf16), turned, turned)
    results = pl.pallas_call(
        functools.partial(kernel, na, nd, rows),
        out_shape=shapes,
        in_specs=[in_hbm] * 3 + [in_smem],
        out_specs=(anywhere,) * 3,
        scratch_shapes=scratch,
        compiler_params=pltpu.CompilerParams(
            collective_id=0, has_side_effects=True, vmem_limit_bytes=47 * 2**20
        ),
    )(local, outer, jnp.swapaxes(momentum, 1, 2), tokens)
    new_weights, grad, updated = results
    grad, updated = jnp.swapaxes(grad, 1, 2), jnp.swapaxes(updated, 1, 2)
    divisor = step_no[0].astype(f32) + 1.0
    return new_weights, 0.9 * momentum + grad, swa + (updated - swa) / divisor


def solution(mesh):
    return jax.shard_map(
        per_device,
        mesh=mesh,
        in_specs=(
            P("rep", None, "fsdp", None),
            P(None, "fsdp", None),
            P(None, "fsdp", "rep"),
            P(None, "fsdp", "rep"),
            P("rep"),
            P(),
        ),
        out_specs=(P(None, "fsdp", None), P(None, "fsdp", "rep"), P(None, "fsdp", "rep")),
        check_vma=False,
    )
```

```python
import functools

import jax
import jax.numpy as jnp
from jax import lax
from jax.experimental import pallas as pl
from jax.experimental.pallas import tpu as pltpu
from jax.sharding import PartitionSpec as P

MESH = pl.DeviceIdType.MESH
NY, NZ, NX = 4, 8, 2
LANES = 128
R = 16
AHEAD = 3
NB = 4
ND = 6
A_AT = (0, 1, 2, 4, 5, 7)
B_AT = (0, 1, 3, 4, 5, 6, 8, 10, 12, 13, 15, 17)
D_AT = (0, 1, 3, 4, 5, 7, 9, 11, 13)
ORDER = (
    ("D", 2), ("B", 2), ("A", 0), ("B", 11), ("B", 10), ("B", 8), ("D", 7), ("A", 3), ("D", 6), ("D", 8), ("D", 3), ("B", 3), ("D", 0), ("D", 5), ("B", 9), ("B", 4), ("A", 5), ("D", 4), ("B", 0), ("A", 1), ("B", 5), ("B", 6), ("B", 7), ("A", 4), ("D", 1), ("A", 2), ("B", 1),
)
RAW, RING, MID, FIRST, SECOND, LAST = 0, 1, 5, 6, 7, 8
XSUM, TREE = 1, 2


def kernel(
    na, nd, rows,
    local, outer, mom_t, tokens,
    out, grad_t, upd_t,
    a_raw, a_own, a_out, a_p, a_x, a_t, a_u, a_v, b_p, a_r, a_q, a_qx, b_w, b_stage,
    d_raw, d_own, d_out, d_p, d_r, d_q, d_qy, d_v,
    cnt, cnt_z, cnt_x, total, gbuf, ubuf, mfull, gfull, ufull, ofull,
    a_ss, b_ss, a_rs, d_ss, d_rs, c_ss, c_rs, m_ss, m_rs, l_sem, o_sem, v_sem, end_s,
):
    f32, bf16 = jnp.float32, jnp.bfloat16
    rep, fsdp = lax.axis_index("rep"), lax.axis_index("fsdp")
    y, z, x = rep // (NZ * NX), (rep // NX) % NZ, rep % NX
    other = 1 - x
    d_row = na * R

    def at(yy, zz, xx):
        return ((lax.rem(yy + 2 * NY, NY) * NZ + lax.rem(zz + 2 * NZ, NZ)) * NX + xx, fsdp)

    def zi(k):
        return lax.rem(z + k + 2 * NZ, NZ)

    def yi(k):
        return lax.rem(y + k + 2 * NY, NY)

    def send(src, dst, ss, rs, where):
        pltpu.make_async_remote_copy(
            src_ref=src, dst_ref=dst, send_sem=ss, recv_sem=rs, device_id=where, device_id_type=MESH
        ).start()

    def drain(ref, sem):
        pltpu.make_async_copy(ref, ref, sem).wait()

    partner = at(y, z, other)
    y_peers = [at(y + k, z, x) for k in range(1, NY)]
    z_peers = [at(y, z + k, x) for k in range(1, NZ)]

    def a_rows(c):
        return pl.ds(pl.multiple_of(c * R, R), R)

    def d_rows(c):
        return pl.ds(pl.multiple_of(d_row + c * R, R), R)

    def lanes(block):
        return pl.ds(block * LANES, LANES)

    def cnt_f(k):
        return cnt[k, 0:1, :].astype(f32)

    half = pl.ds(pl.multiple_of(x * (LANES // 2), LANES // 2), LANES // 2)
    other_half = pl.ds(pl.multiple_of(other * (LANES // 2), LANES // 2), LANES // 2)
    ycols = pl.ds(pl.multiple_of(y * (NZ * LANES), NZ * LANES), NZ * LANES)
    cols = pl.ds(pl.multiple_of((y * NZ + z) * LANES, LANES), LANES)
    arows, drows = pl.ds(0, na * R), pl.ds(d_row, nd * R)
    loads = [
        pltpu.make_async_copy(local.at[0, :, arows, ycols], a_own, l_sem.at[1]),
        pltpu.make_async_copy(outer.at[:, arows, ycols], a_out, l_sem.at[2]),
        pltpu.make_async_copy(local.at[0, x, drows, :], d_own, l_sem.at[3]),
        pltpu.make_async_copy(outer.at[x, drows, :], d_out, l_sem.at[4]),
    ]
    late_loads = [
        pltpu.make_async_copy(outer.at[x, :, cols], ofull, l_sem.at[0]),
        pltpu.make_async_copy(mom_t.at[x], gbuf.at[half], l_sem.at[5]),
    ]
    for load in loads + late_loads:
        load.start()
    cnt[0] = jnp.full((8, LANES), tokens[0], jnp.int32)

    barrier = pltpu.get_barrier_semaphore()
    peers = y_peers + z_peers + [partner]
    for peer in peers:
        pl.semaphore_signal(barrier, inc=1, device_id=peer, device_id_type=MESH)
    pl.semaphore_wait(barrier, len(peers))

    def send_raw(c):
        @pl.when(c < na)
        def _():
            for k in (2, 1, 3):
                theirs = pl.ds(pl.multiple_of(yi(k) * (NZ * LANES), NZ * LANES), NZ * LANES)
                send(
                    local.at[0, :, a_rows(c), theirs], a_raw.at[c, k - 1],
                    a_ss.at[RAW], a_rs.at[c, RAW], y_peers[k - 1],
                )

        @pl.when(c < nd)
        def _():
            send(local.at[0, other, d_rows(c), :], d_raw.at[c], d_ss.at[RAW], d_rs.at[c, RAW], partner)

    def ring_stage(stage, c, sign, p, r, ss, rs):
        up, down = at(y, z + sign, x), at(y, z - sign, x)

        def step(k, long, short):
            send(long, r.at[c, k, 0], ss.at[RING + k], rs.at[c, RING + k], up)
            if k < 3:
                send(short, r.at[c, k, 1], ss.at[RING + k], rs.at[c, RING + k], down)

        if stage == 0:
            step(0, p.at[c, zi(4 * sign)], p.at[c, zi(-3 * sign)])
            return
        k = stage - 1
        came = r.at[c, k] if k < 3 else r.at[c, k, 0]
        drain(came, rs.at[c, RING + k])
        if k < 3:
            r[c, k, 0] += p[c, zi((3 - k) * sign)]
            if k < 2:
                r[c, k, 1] += p[c, zi(-(2 - k) * sign)]
            step(k + 1, r.at[c, k, 0], r.at[c, k, 1])

    def update(rws, pg_sum):
        o = ofull[rws, :].astype(f32)
        pg = pg_sum / total[0:1, :]
        upd = o - 0.7 * (pg + 0.9 * (0.9 * mfull[rws, :] + pg))
        gfull[rws, :] = pg
        ufull[rws, :] = upd
        return upd.astype(bf16)

    def a_sums(c):
        drain(a_raw.at[c], a_rs.at[c, RAW])
        for zz in range(NZ):
            for m in range(2):
                o = a_out[m, a_rows(c), lanes(zz)].astype(f32)
                acc = cnt_f(0) * (o - a_own[m, a_rows(c), lanes(zz)].astype(f32))
                for k in range(1, NY):
                    acc += cnt_f(k) * (o - a_raw[c, k - 1, m, :, lanes(zz)].astype(f32))
                a_p[c, m, zz] = acc

    def a_stage_fn(stage, c):
        e = c - NB
        sign = 1 - 2 * (c % 2)

        def sems(k):
            return a_ss.at[k], a_rs.at[c, k]

        def landed(ref, k):
            drain(ref, a_rs.at[c, k])

        if stage == 0:
            a_sums(c)
            send(a_p.at[c, other], a_x.at[e], *sems(XSUM), partner)
        elif stage == 1:
            landed(a_x.at[e], XSUM)
            a_x[e] += a_p[c, x]
            send(a_x.at[e, zi(4 * sign)], a_t.at[e, 0], *sems(TREE), at(y, z + 2 * sign, x))
            send(a_x.at[e, zi(3 * sign)], a_t.at[e, 1], *sems(TREE), at(y, z + sign, x))
            send(a_x.at[e, zi(-3 * sign)], a_t.at[e, 2], *sems(TREE), at(y, z - sign, x))
        elif stage == 2:
            landed(a_t.at[e], TREE)
            a_t[e, 0] += a_t[e, 1] + a_x[e, zi(2 * sign)]
            a_t[e, 2] += a_x[e, zi(-2 * sign)]
            send(a_t.at[e, 0], a_u.at[e, 0], *sems(TREE + 1), at(y, z + 2 * sign, x))
            send(a_t.at[e, 2], a_u.at[e, 1], *sems(TREE + 1), at(y, z - 2 * sign, x))
            send(a_x.at[e, zi(sign)], a_u.at[e, 2], *sems(TREE + 1), at(y, z + sign, x))
            send(a_x.at[e, zi(-sign)], a_u.at[e, 3], *sems(TREE + 1), at(y, z - sign, x))
        elif stage == 3:
            landed(a_u.at[e], TREE + 1)
            a_v[e] = update(a_rows(c), a_x[e, z] + ((a_u[e, 0] + a_u[e, 1]) + (a_u[e, 2] + a_u[e, 3])))
            place = out.at[x, a_rows(c), cols]
            pltpu.make_async_copy(a_v.at[e], place, v_sem.at[0, c % 4]).start()
            for k in (4, 3, 5, 2, 6, 1, 7):
                send(a_v.at[e], place, *sems(FIRST), z_peers[k - 1])
        elif stage == 4:
            landed(out.at[x, a_rows(c), pl.ds(0, (NZ - 1) * LANES)], FIRST)
            drain(a_v.at[e], v_sem.at[0, c % 4])
            place = out.at[x, a_rows(c), ycols]
            for k in (2, 1, 3):
                send(place, place, *sems(SECOND), y_peers[k - 1])
        else:
            landed(out.at[x, a_rows(c), pl.ds(0, (NY - 1) * NZ * LANES)], SECOND)
            place = out.at[x, a_rows(c), :]
            send(place, place, a_ss.at[LAST], end_s.at[0], partner)

    def b_stage_fn(stage, c):
        sign = 1 - 2 * (c % 2)
        up, down = at(y, z + sign, x), at(y, z - sign, x)

        def sems(k):
            return b_ss.at[k], a_rs.at[c, k]

        def landed(ref, k):
            drain(ref, a_rs.at[c, k])

        def step(k):
            long, short = b_w.at[c, zi(-k * sign)], b_w.at[c, zi(k * sign)]
            send(long, long, *sems(LAST + k), up)
            if k < 3:
                send(short, short, *sems(LAST + k), down)

        ring = functools.partial(ring_stage, c=c, sign=sign, p=b_p, r=a_r, ss=b_ss, rs=a_rs)
        if stage == 0:
            a_sums(c)
            for zz in range(NZ):
                for m in range(2):
                    b_p[c, zz, m] = a_p[c, m, zz]
            ring(0)
        elif stage <= 3:
            ring(stage)
        elif stage == 4:
            ring(4)
            a_q[c] = b_p[c, z] + a_r[c, 3, 0] + a_r[c, 2, 1]
            send(a_q.at[c, other], a_qx.at[c], *sems(MID), partner)
        elif stage == 5:
            landed(a_qx.at[c], MID)
            mine = b_w.at[c, z, y, x]
            mine[...] = update(a_rows(c), a_q[c, x] + a_qx[c])
            send(mine, mine, *sems(FIRST), partner)
        elif stage == 6:
            landed(b_w.at[c, z, y, other], FIRST)
            mine = b_w.at[c, z, y]
            for k in (2, 1, 3):
                send(mine, mine, *sems(SECOND), y_peers[k - 1])
        elif stage == 7:
            landed(b_w.at[c, z, pl.ds(0, NY - 1)], SECOND)
            step(0)
        else:
            k = stage - 8
            came = b_w.at[c, pl.ds(0, 2 if k < 3 else 1)]
            landed(came, LAST + k)
            if k < 3:
                step(k + 1)
            else:
                for yy in range(NY):
                    for zz in range(NZ):
                        for m in range(2):
                            b_stage[c, m, :, lanes(yy * NZ + zz)] = b_w[c, zz, yy, m]
                pltpu.make_async_copy(b_stage.at[c], out.at[:, a_rows(c), :], o_sem).start()

    def d_stage_fn(stage, c):
        ring = functools.partial(ring_stage, c=c, sign=2 * (c % 2) - 1, p=d_p, r=d_r, ss=d_ss, rs=d_rs)

        def sems(k):
            return d_ss.at[k], d_rs.at[c, k]

        def landed(ref, k):
            drain(ref, d_rs.at[c, k])

        if stage == 0:
            landed(d_raw.at[c], RAW)
            own = pl.ds(pl.multiple_of(c * R, R), R)
            for yy in range(NY):
                for zz in range(NZ):
                    sl = lanes(yy * NZ + zz)
                    o = d_out[own, sl].astype(f32)
                    mine = cnt_f(0) * (o - d_own[own, sl].astype(f32))
                    d_p[c, zz, yy] = mine + cnt_f(NY) * (o - d_raw[c, :, sl].astype(f32))
            ring(0)
        elif stage <= 3:
            ring(stage)
        elif stage == 4:
            ring(4)
            d_q[c] = d_p[c, z] + d_r[c, 3, 0] + d_r[c, 2, 1]
            for k in (2, 1, 3):
                send(d_q.at[c, yi(k)], d_qy.at[c, k - 1], *sems(MID), y_peers[k - 1])
        elif stage == 5:
            landed(d_qy.at[c], MID)
            d_v[c] = update(d_rows(c), d_q[c, y] + d_qy[c, 0] + d_qy[c, 1] + d_qy[c, 2])
            place = out.at[x, d_rows(c), cols]
            pltpu.make_async_copy(d_v.at[c], place, v_sem.at[1, c % 4]).start()
            for k in (4, 3, 5, 2, 6, 1, 7):
                send(d_v.at[c], place, *sems(FIRST), z_peers[k - 1])
        elif stage == 6:
            landed(out.at[x, d_rows(c), pl.ds(0, (NZ - 1) * LANES)], FIRST)
            drain(d_v.at[c], v_sem.at[1, c % 4])
            place = out.at[x, d_rows(c), ycols]
            send(place, place, *sems(SECOND), partner)
        elif stage == 7:
            landed(out.at[other, d_rows(c), ycols], SECOND)
            place = out.at[:, d_rows(c), ycols]
            for k in (1, 3):
                send(place, place, *sems(LAST), y_peers[k - 1])
        else:
            landed(out.at[:, d_rows(c), pl.ds(0, 2 * NZ * LANES)], LAST)
            for k, m in ((1, 0), (-1, 1)):
                theirs = pl.ds(pl.multiple_of(yi(-k) * (NZ * LANES), NZ * LANES), NZ * LANES)
                place = out.at[m, d_rows(c), theirs]
                send(place, place, d_ss.at[LAST + 1], end_s.at[1], at(y + k, z, x))

    send_raw(0)
    for k in range(1, NY):
        send(cnt.at[0], cnt.at[k], c_ss.at[0], c_rs.at[0], y_peers[k - 1])
    send(cnt.at[0], cnt.at[NY], c_ss.at[0], c_rs.at[0], partner)
    for c in range(1, AHEAD):
        send_raw(c)
    drain(cnt.at[pl.ds(0, NY)], c_rs.at[0])
    drain(cnt.at[pl.ds(0, NY)], c_ss.at[0])
    cnt_z[0] = cnt[0] + cnt[1] + cnt[2] + cnt[3]
    for k in range(1, NZ):
        send(cnt_z.at[0], cnt_z.at[k], c_ss.at[1], c_rs.at[1], z_peers[k - 1])
    for load in loads:
        load.wait()

    def slot(t, carry):
        @pl.when(t == 2)
        def _():
            drain(cnt_z.at[pl.ds(0, NZ - 1)], c_rs.at[1])
            drain(cnt_z.at[pl.ds(0, NZ - 1)], c_ss.at[1])
            acc = cnt_z[0]
            for k in range(1, NZ):
                acc += cnt_z[k]
            cnt_x[0] = acc
            send(cnt_x.at[0], cnt_x.at[1], c_ss.at[2], c_rs.at[2], partner)
            send(mom_t.at[other], gbuf.at[half], m_ss.at[0], m_rs.at[0], partner)

        @pl.when(t == 5)
        def _():
            drain(cnt_x.at[0], c_rs.at[2])
            drain(cnt_x.at[0], c_ss.at[2])
            total[...] = (cnt_x[0] + cnt_x[1]).astype(f32)
            drain(gbuf.at[other_half], m_rs.at[0])
            drain(gbuf.at[other_half], m_ss.at[0])
            for load in late_loads:
                load.wait()
            mfull[...] = gbuf[...].T

        for kind, stage in ORDER:
            if kind == "D":
                c, low, high, fn = t - D_AT[stage], 0, nd, d_stage_fn
            elif kind == "B":
                c, low, high, fn = t - B_AT[stage], 0, NB, b_stage_fn
            else:
                c, low, high, fn = t - A_AT[stage], NB, na, a_stage_fn
            pl.when((c >= low) & (c < high))(functools.partial(fn, stage, c))
        send_raw(t + AHEAD)

        @pl.when(t == max(na + A_AT[3], NB + B_AT[5], nd + D_AT[5]))
        def _():
            gbuf[...] = gfull[...].T
            ubuf[...] = ufull[...].T
            send(gbuf.at[other_half], grad_t.at[x], m_ss.at[0], m_rs.at[0], partner)
            send(ubuf.at[other_half], upd_t.at[x], m_ss.at[1], m_rs.at[1], partner)
            pltpu.make_async_copy(gbuf.at[half], grad_t.at[x], l_sem.at[5]).start()
            pltpu.make_async_copy(ubuf.at[half], upd_t.at[x], l_sem.at[6]).start()

        return carry

    lax.fori_loop(0, max(na + A_AT[-1], NB + B_AT[-1], nd + D_AT[-1]), slot, 0)
    pltpu.make_async_copy(gbuf.at[half], grad_t.at[x], l_sem.at[5]).wait()
    pltpu.make_async_copy(ubuf.at[half], upd_t.at[x], l_sem.at[6]).wait()
    drain(grad_t.at[other], m_rs.at[0])
    drain(upd_t.at[other], m_rs.at[1])
    drain(gbuf.at[other_half], m_ss.at[0])
    drain(ubuf.at[other_half], m_ss.at[1])

    def part(mats, chunks, blocks):
        return out.at[pl.ds(0, mats), pl.ds(0, chunks * R), pl.ds(0, blocks * LANES)]

    for ref, sem in [
        (part(1, na - NB, NY * NZ), end_s.at[0]), (part(1, nd, 2 * NZ), end_s.at[1]), (part(2, NB, NY * NZ), o_sem),
        (a_raw, a_ss.at[RAW]), (a_x, a_ss.at[XSUM]), (a_t, a_ss.at[TREE]), (a_u, a_ss.at[TREE + 1]),
        (a_r.at[:, 3, 0], b_ss.at[RING + 3]), (a_qx, b_ss.at[MID]),
        (part(1, na - NB, NZ - 1), a_ss.at[FIRST]), (part(1, na - NB, (NY - 1) * NZ), a_ss.at[SECOND]),
        (part(1, na - NB, NY * NZ), a_ss.at[LAST]),
        (b_w.at[:, 0, 0, 0], b_ss.at[FIRST]), (b_w.at[:, 0, pl.ds(0, NY - 1)], b_ss.at[SECOND]),
        (b_w.at[:, 0], b_ss.at[LAST + 3]),
        (d_raw, d_ss.at[RAW]), (d_r.at[:, 3, 0], d_ss.at[RING + 3]), (d_qy, d_ss.at[MID]),
        (part(1, nd, NZ - 1), d_ss.at[FIRST]), (part(1, nd, NZ), d_ss.at[SECOND]),
        (part(2, nd, 2 * NZ), d_ss.at[LAST]), (part(1, nd, 2 * NZ), d_ss.at[LAST + 1]),
    ]:
        drain(ref, sem)
    for k in range(3):
        drain(a_r.at[:, k], b_ss.at[RING + k])
        drain(b_w.at[:, pl.ds(0, 2)], b_ss.at[LAST + k])
        drain(d_r.at[:, k], d_ss.at[RING + k])


def per_device(local, outer, momentum, swa, tokens, step_no):
    mats, rows, width = outer.shape
    nd = ND
    na = rows // R - nd
    f32, bf16, i32 = jnp.float32, jnp.bfloat16, jnp.int32
    vmem, dma = pltpu.VMEM, pltpu.SemaphoreType.DMA
    wide = NZ * LANES
    scratch = [
        vmem((na, NY - 1, mats, R, wide), bf16),
        vmem((mats, na * R, wide), bf16),
        vmem((mats, na * R, wide), bf16),
        vmem((na, mats, NZ, R, LANES), f32),
        vmem((na - NB, NZ, R, LANES), f32),
        vmem((na - NB, 3, R, LANES), f32),
        vmem((na - NB, 4, R, LANES), f32),
        vmem((na - NB, R, LANES), bf16),
        vmem((NB, NZ, mats, R, LANES), f32),
        vmem((NB, 4, 2, mats, R, LANES), f32),
        vmem((NB, mats, R, LANES), f32),
        vmem((NB, R, LANES), f32),
        vmem((NB, NZ, NY, NX, R, LANES), bf16),
        vmem((NB, mats, R, width), bf16),
        vmem((nd, R, width), bf16),
        vmem((nd * R, width), bf16),
        vmem((nd * R, width), bf16),
        vmem((nd, NZ, NY, R, LANES), f32),
        vmem((nd, 4, 2, NY, R, LANES), f32),
        vmem((nd, NY, R, LANES), f32),
        vmem((nd, NY - 1, R, LANES), f32),
        vmem((nd, R, LANES), bf16),
        vmem((NY + 1, 8, LANES), i32),
        vmem((NZ, 8, LANES), i32),
        vmem((2, 8, LANES), i32),
        vmem((8, LANES), f32),
        vmem((LANES, rows), f32),
        vmem((LANES, rows), f32),
        vmem((rows, LANES), f32),
        vmem((rows, LANES), f32),
        vmem((rows, LANES), f32),
        vmem((rows, LANES), bf16),
        dma((9,)), dma((12,)), dma((na, 12)), dma((10,)), dma((nd, 10)),
        dma((3,)), dma((3,)), dma((2,)), dma((2,)), dma((7,)), dma, dma((2, 4)), dma((2,)),
    ]
    anywhere = pl.BlockSpec(memory_space=pl.ANY)
    in_hbm = pl.BlockSpec(memory_space=pltpu.HBM)
    in_smem = pl.BlockSpec(memory_space=pltpu.SMEM)
    turned = jax.ShapeDtypeStruct((mats, LANES // 2, rows), f32)
    shapes = (jax.ShapeDtypeStruct(outer.shape, bf16), turned, turned)
    results = pl.pallas_call(
        functools.partial(kernel, na, nd, rows),
        out_shape=shapes,
        in_specs=[in_hbm] * 3 + [in_smem],
        out_specs=(anywhere,) * 3,
        scratch_shapes=scratch,
        compiler_params=pltpu.CompilerParams(
            collective_id=0, has_side_effects=True, vmem_limit_bytes=47 * 2**20
        ),
    )(local, outer, jnp.swapaxes(momentum, 1, 2), tokens)
    new_weights, grad, updated = results
    grad, updated = jnp.swapaxes(grad, 1, 2), jnp.swapaxes(updated, 1, 2)
    divisor = step_no[0].astype(f32) + 1.0
    return new_weights, 0.9 * momentum + grad, swa + (updated - swa) / divisor


def solution(mesh):
    return jax.shard_map(
        per_device,
        mesh=mesh,
        in_specs=(
            P("rep", None, "fsdp", None),
            P(None, "fsdp", None),
            P(None, "fsdp", "rep"),
            P(None, "fsdp", "rep"),
            P("rep"),
            P(),
        ),
        out_specs=(P(None, "fsdp", None), P(None, "fsdp", "rep"), P(None, "fsdp", "rep")),
        check_vma=False,
    )
```

```python
import functools

import jax
import jax.numpy as jnp
from jax import lax
from jax.experimental import pallas as pl
from jax.experimental.pallas import tpu as pltpu
from jax.sharding import PartitionSpec as P

MESH = pl.DeviceIdType.MESH
NY, NZ, NX = 4, 8, 2
LANES = 128
R = 16
AHEAD = 3
NB = 4
ND = 6
A_AT = (0, 1, 2, 4, 5, 7)
B_AT = (0, 1, 3, 4, 5, 6, 8, 10, 12, 13, 15, 17)
D_AT = (0, 1, 3, 4, 5, 7, 9, 11, 13)
ORDER = (
    ("D", 2), ("B", 2), ("A", 0), ("B", 11), ("B", 10), ("B", 8), ("D", 7), ("A", 3), ("D", 6), ("D", 8), ("D", 3), ("B", 3), ("D", 0), ("D", 5), ("B", 9), ("B", 4), ("A", 5), ("D", 4), ("B", 0), ("A", 1), ("B", 5), ("B", 6), ("B", 7), ("A", 4), ("D", 1), ("A", 2), ("B", 1),
)
RAW, RING, MID, FIRST, SECOND, LAST = 0, 1, 5, 6, 7, 8
XSUM, TREE = 1, 2


def kernel(
    na, nd, rows,
    local, outer, mom_t, tokens,
    out, grad_t, upd_t,
    a_raw, a_own, a_out, a_p, a_x, a_t, a_u, a_v, b_p, a_r, a_q, a_qx, b_w, b_stage,
    d_raw, d_own, d_out, d_p, d_r, d_q, d_qy, d_v,
    cnt, cnt_z, cnt_x, total, gbuf, ubuf, mfull, gfull, ufull, ofull,
    a_ss, b_ss, a_rs, b_rs, d_ss, d_rs, c_ss, c_rs, m_ss, m_rs, l_sem, o_sem, v_sem, end_s,
):
    f32, bf16 = jnp.float32, jnp.bfloat16
    rep, fsdp = lax.axis_index("rep"), lax.axis_index("fsdp")
    y, z, x = rep // (NZ * NX), (rep // NX) % NZ, rep % NX
    other = 1 - x
    d_row = na * R

    def at(yy, zz, xx):
        return ((lax.rem(yy + 2 * NY, NY) * NZ + lax.rem(zz + 2 * NZ, NZ)) * NX + xx, fsdp)

    def zi(k):
        return lax.rem(z + k + 2 * NZ, NZ)

    def yi(k):
        return lax.rem(y + k + 2 * NY, NY)

    def send(src, dst, ss, rs, where):
        pltpu.make_async_remote_copy(
            src_ref=src, dst_ref=dst, send_sem=ss, recv_sem=rs, device_id=where, device_id_type=MESH
        ).start()

    def drain(ref, sem):
        pltpu.make_async_copy(ref, ref, sem).wait()

    partner = at(y, z, other)
    y_peers = [at(y + k, z, x) for k in range(1, NY)]
    z_peers = [at(y, z + k, x) for k in range(1, NZ)]

    def a_rows(c):
        return pl.ds(pl.multiple_of(c * R, R), R)

    def d_rows(c):
        return pl.ds(pl.multiple_of(d_row + c * R, R), R)

    def lanes(block):
        return pl.ds(block * LANES, LANES)

    def cnt_f(k):
        return cnt[k, 0:1, :].astype(f32)

    half = pl.ds(pl.multiple_of(x * (LANES // 2), LANES // 2), LANES // 2)
    other_half = pl.ds(pl.multiple_of(other * (LANES // 2), LANES // 2), LANES // 2)
    ycols = pl.ds(pl.multiple_of(y * (NZ * LANES), NZ * LANES), NZ * LANES)
    cols = pl.ds(pl.multiple_of((y * NZ + z) * LANES, LANES), LANES)
    arows, drows = pl.ds(0, na * R), pl.ds(d_row, nd * R)
    loads = [
        pltpu.make_async_copy(local.at[0, :, arows, ycols], a_own, l_sem.at[1]),
        pltpu.make_async_copy(outer.at[:, arows, ycols], a_out, l_sem.at[2]),
        pltpu.make_async_copy(local.at[0, x, drows, :], d_own, l_sem.at[3]),
        pltpu.make_async_copy(outer.at[x, drows, :], d_out, l_sem.at[4]),
    ]
    late_loads = [
        pltpu.make_async_copy(outer.at[x, :, cols], ofull, l_sem.at[0]),
        pltpu.make_async_copy(mom_t.at[x], gbuf.at[half], l_sem.at[5]),
    ]
    for load in loads + late_loads:
        load.start()
    cnt[0] = jnp.full((8, LANES), tokens[0], jnp.int32)

    barrier = pltpu.get_barrier_semaphore()
    peers = y_peers + z_peers + [partner]
    for peer in peers:
        pl.semaphore_signal(barrier, inc=1, device_id=peer, device_id_type=MESH)
    pl.semaphore_wait(barrier, len(peers))

    def send_raw(c):
        @pl.when(c < na)
        def _():
            for k in (2, 1, 3):
                theirs = pl.ds(pl.multiple_of(yi(k) * (NZ * LANES), NZ * LANES), NZ * LANES)
                send(
                    local.at[0, :, a_rows(c), theirs], a_raw.at[c, k - 1],
                    a_ss.at[RAW], a_rs.at[c, RAW], y_peers[k - 1],
                )

        @pl.when(c < nd)
        def _():
            send(local.at[0, other, d_rows(c), :], d_raw.at[c], d_ss.at[RAW], d_rs.at[c, RAW], partner)

    def ring_stage(stage, c, sign, p, r, ss, rs):
        up, down = at(y, z + sign, x), at(y, z - sign, x)

        def step(k, long, short):
            send(long, r.at[c, k, 0], ss.at[RING + k], rs.at[c, RING + k], up)
            if k < 3:
                send(short, r.at[c, k, 1], ss.at[RING + k], rs.at[c, RING + k], down)

        if stage == 0:
            step(0, p.at[c, zi(4 * sign)], p.at[c, zi(-3 * sign)])
            return
        k = stage - 1
        came = r.at[c, k] if k < 3 else r.at[c, k, 0]
        drain(came, rs.at[c, RING + k])
        if k < 3:
            r[c, k, 0] += p[c, zi((3 - k) * sign)]
            if k < 2:
                r[c, k, 1] += p[c, zi(-(2 - k) * sign)]
            step(k + 1, r.at[c, k, 0], r.at[c, k, 1])

    def update(rws, pg_sum):
        o = ofull[rws, :].astype(f32)
        pg = pg_sum / total[0:1, :]
        upd = o - 0.7 * (pg + 0.9 * (0.9 * mfull[rws, :] + pg))
        gfull[rws, :] = pg
        ufull[rws, :] = upd
        return upd.astype(bf16)

    def a_sums(c, keep):
        drain(a_raw.at[c], a_rs.at[c, RAW])
        for zz in range(NZ):
            for m in range(2):
                o = a_out[m, a_rows(c), lanes(zz)].astype(f32)
                acc = cnt_f(0) * (o - a_own[m, a_rows(c), lanes(zz)].astype(f32))
                for k in range(1, NY):
                    acc += cnt_f(k) * (o - a_raw[c, k - 1, m, :, lanes(zz)].astype(f32))
                keep(m, zz, acc)

    def a_stage_fn(stage, c):
        e = c - NB
        sign = 1 - 2 * (c % 2)

        def sems(k):
            return a_ss.at[k], a_rs.at[c, k]

        def landed(ref, k):
            drain(ref, a_rs.at[c, k])

        if stage == 0:
            def keep(m, zz, acc):
                a_p[e, m, zz] = acc

            a_sums(c, keep)
            send(a_p.at[e, other], a_x.at[e], *sems(XSUM), partner)
        elif stage == 1:
            landed(a_x.at[e], XSUM)
            a_x[e] += a_p[e, x]
            send(a_x.at[e, zi(4 * sign)], a_t.at[e, 0], *sems(TREE), at(y, z + 2 * sign, x))
            send(a_x.at[e, zi(3 * sign)], a_t.at[e, 1], *sems(TREE), at(y, z + sign, x))
            send(a_x.at[e, zi(-3 * sign)], a_t.at[e, 2], *sems(TREE), at(y, z - sign, x))
        elif stage == 2:
            landed(a_t.at[e], TREE)
            a_t[e, 0] += a_t[e, 1] + a_x[e, zi(2 * sign)]
            a_t[e, 2] += a_x[e, zi(-2 * sign)]
            send(a_t.at[e, 0], a_u.at[e, 0], *sems(TREE + 1), at(y, z + 2 * sign, x))
            send(a_t.at[e, 2], a_u.at[e, 1], *sems(TREE + 1), at(y, z - 2 * sign, x))
            send(a_x.at[e, zi(sign)], a_u.at[e, 2], *sems(TREE + 1), at(y, z + sign, x))
            send(a_x.at[e, zi(-sign)], a_u.at[e, 3], *sems(TREE + 1), at(y, z - sign, x))
        elif stage == 3:
            landed(a_u.at[e], TREE + 1)
            a_v[e] = update(a_rows(c), a_x[e, z] + ((a_u[e, 0] + a_u[e, 1]) + (a_u[e, 2] + a_u[e, 3])))
            place = out.at[x, a_rows(c), cols]
            pltpu.make_async_copy(a_v.at[e], place, v_sem.at[0, c % 4]).start()
            for k in (4, 3, 5, 2, 6, 1, 7):
                send(a_v.at[e], place, *sems(FIRST), z_peers[k - 1])
        elif stage == 4:
            landed(out.at[x, a_rows(c), pl.ds(0, (NZ - 1) * LANES)], FIRST)
            drain(a_v.at[e], v_sem.at[0, c % 4])
            place = out.at[x, a_rows(c), ycols]
            for k in (2, 1, 3):
                send(place, place, *sems(SECOND), y_peers[k - 1])
        else:
            landed(out.at[x, a_rows(c), pl.ds(0, (NY - 1) * NZ * LANES)], SECOND)
            place = out.at[x, a_rows(c), :]
            send(place, place, a_ss.at[LAST], end_s.at[0], partner)

    def b_stage_fn(stage, c):
        sign = 1 - 2 * (c % 2)
        up, down = at(y, z + sign, x), at(y, z - sign, x)

        def sems(k):
            return b_ss.at[k], a_rs.at[c, k]

        def landed(ref, k):
            drain(ref, a_rs.at[c, k])

        def step(k):
            long, short = b_w.at[c, zi(-k * sign)], b_w.at[c, zi(k * sign)]
            send(long, long, b_ss.at[LAST + k], b_rs.at[c, k], up)
            if k < 3:
                send(short, short, b_ss.at[LAST + k], b_rs.at[c, k], down)

        ring = functools.partial(ring_stage, c=c, sign=sign, p=b_p, r=a_r, ss=b_ss, rs=a_rs)
        if stage == 0:

            def keep(m, zz, acc):
                b_p[c, zz, m] = acc

            a_sums(c, keep)
            ring(0)
        elif stage <= 3:
            ring(stage)
        elif stage == 4:
            ring(4)
            a_q[c] = b_p[c, z] + a_r[c, 3, 0] + a_r[c, 2, 1]
            send(a_q.at[c, other], a_qx.at[c], *sems(MID), partner)
        elif stage == 5:
            landed(a_qx.at[c], MID)
            mine = b_w.at[c, z, y, x]
            mine[...] = update(a_rows(c), a_q[c, x] + a_qx[c])
            send(mine, mine, *sems(FIRST), partner)
        elif stage == 6:
            landed(b_w.at[c, z, y, other], FIRST)
            mine = b_w.at[c, z, y]
            for k in (2, 1, 3):
                send(mine, mine, *sems(SECOND), y_peers[k - 1])
        elif stage == 7:
            landed(b_w.at[c, z, pl.ds(0, NY - 1)], SECOND)
            step(0)
        else:
            k = stage - 8
            came = b_w.at[c, pl.ds(0, 2 if k < 3 else 1)]
            drain(came, b_rs.at[c, k])
            if k < 3:
                step(k + 1)
            else:
                for yy in range(NY):
                    for zz in range(NZ):
                        for m in range(2):
                            b_stage[c, m, :, lanes(yy * NZ + zz)] = b_w[c, zz, yy, m]
                pltpu.make_async_copy(b_stage.at[c], out.at[:, a_rows(c), :], o_sem).start()

    def d_stage_fn(stage, c):
        ring = functools.partial(ring_stage, c=c, sign=2 * (c % 2) - 1, p=d_p, r=d_r, ss=d_ss, rs=d_rs)

        def sems(k):
            return d_ss.at[k], d_rs.at[c, k]

        def landed(ref, k):
            drain(ref, d_rs.at[c, k])

        if stage == 0:
            landed(d_raw.at[c], RAW)
            own = pl.ds(pl.multiple_of(c * R, R), R)
            for yy in range(NY):
                for zz in range(NZ):
                    sl = lanes(yy * NZ + zz)
                    o = d_out[own, sl].astype(f32)
                    mine = cnt_f(0) * (o - d_own[own, sl].astype(f32))
                    d_p[c, zz, yy] = mine + cnt_f(NY) * (o - d_raw[c, :, sl].astype(f32))
            ring(0)
        elif stage <= 3:
            ring(stage)
        elif stage == 4:
            ring(4)
            d_q[c] = d_p[c, z] + d_r[c, 3, 0] + d_r[c, 2, 1]
            for k in (2, 1, 3):
                send(d_q.at[c, yi(k)], d_qy.at[c, k - 1], *sems(MID), y_peers[k - 1])
        elif stage == 5:
            landed(d_qy.at[c], MID)
            d_v[c] = update(d_rows(c), d_q[c, y] + d_qy[c, 0] + d_qy[c, 1] + d_qy[c, 2])
            place = out.at[x, d_rows(c), cols]
            pltpu.make_async_copy(d_v.at[c], place, v_sem.at[1, c % 4]).start()
            for k in (4, 3, 5, 2, 6, 1, 7):
                send(d_v.at[c], place, *sems(FIRST), z_peers[k - 1])
        elif stage == 6:
            landed(out.at[x, d_rows(c), pl.ds(0, (NZ - 1) * LANES)], FIRST)
            drain(d_v.at[c], v_sem.at[1, c % 4])
            place = out.at[x, d_rows(c), ycols]
            send(place, place, *sems(SECOND), partner)
        elif stage == 7:
            landed(out.at[other, d_rows(c), ycols], SECOND)
            place = out.at[:, d_rows(c), ycols]
            for k in (1, 3):
                send(place, place, *sems(LAST), y_peers[k - 1])
        else:
            landed(out.at[:, d_rows(c), pl.ds(0, 2 * NZ * LANES)], LAST)
            for k, m in ((1, 0), (-1, 1)):
                theirs = pl.ds(pl.multiple_of(yi(-k) * (NZ * LANES), NZ * LANES), NZ * LANES)
                place = out.at[m, d_rows(c), theirs]
                send(place, place, d_ss.at[LAST + 1], end_s.at[1], at(y + k, z, x))

    send_raw(0)
    for k in range(1, NY):
        send(cnt.at[0], cnt.at[k], c_ss.at[0], c_rs.at[0], y_peers[k - 1])
    send(cnt.at[0], cnt.at[NY], c_ss.at[0], c_rs.at[0], partner)
    for c in range(1, AHEAD):
        send_raw(c)
    drain(cnt.at[pl.ds(0, NY)], c_rs.at[0])
    drain(cnt.at[pl.ds(0, NY)], c_ss.at[0])
    cnt_z[0] = cnt[0] + cnt[1] + cnt[2] + cnt[3]
    for k in range(1, NZ):
        send(cnt_z.at[0], cnt_z.at[k], c_ss.at[1], c_rs.at[1], z_peers[k - 1])
    for load in loads:
        load.wait()

    def slot(t, carry):
        @pl.when(t == 2)
        def _():
            drain(cnt_z.at[pl.ds(0, NZ - 1)], c_rs.at[1])
            drain(cnt_z.at[pl.ds(0, NZ - 1)], c_ss.at[1])
            acc = cnt_z[0]
            for k in range(1, NZ):
                acc += cnt_z[k]
            cnt_x[0] = acc
            send(cnt_x.at[0], cnt_x.at[1], c_ss.at[2], c_rs.at[2], partner)
            send(mom_t.at[other], gbuf.at[half], m_ss.at[0], m_rs.at[0], partner)

        @pl.when(t == 5)
        def _():
            drain(cnt_x.at[0], c_rs.at[2])
            drain(cnt_x.at[0], c_ss.at[2])
            total[...] = (cnt_x[0] + cnt_x[1]).astype(f32)
            drain(gbuf.at[other_half], m_rs.at[0])
            drain(gbuf.at[other_half], m_ss.at[0])
            for load in late_loads:
                load.wait()
            mfull[...] = gbuf[...].T

        for kind, stage in ORDER:
            if kind == "D":
                c, low, high, fn = t - D_AT[stage], 0, nd, d_stage_fn
            elif kind == "B":
                c, low, high, fn = t - B_AT[stage], 0, NB, b_stage_fn
            else:
                c, low, high, fn = t - A_AT[stage], NB, na, a_stage_fn
            pl.when((c >= low) & (c < high))(functools.partial(fn, stage, c))
        send_raw(t + AHEAD)

        @pl.when(t == max(na + A_AT[3], NB + B_AT[5], nd + D_AT[5]))
        def _():
            gbuf[...] = gfull[...].T
            ubuf[...] = ufull[...].T
            send(gbuf.at[other_half], grad_t.at[x], m_ss.at[0], m_rs.at[0], partner)
            send(ubuf.at[other_half], upd_t.at[x], m_ss.at[1], m_rs.at[1], partner)
            pltpu.make_async_copy(gbuf.at[half], grad_t.at[x], l_sem.at[5]).start()
            pltpu.make_async_copy(ubuf.at[half], upd_t.at[x], l_sem.at[6]).start()

        return carry

    lax.fori_loop(0, max(na + A_AT[-1], NB + B_AT[-1], nd + D_AT[-1]), slot, 0)
    pltpu.make_async_copy(gbuf.at[half], grad_t.at[x], l_sem.at[5]).wait()
    pltpu.make_async_copy(ubuf.at[half], upd_t.at[x], l_sem.at[6]).wait()
    drain(grad_t.at[other], m_rs.at[0])
    drain(upd_t.at[other], m_rs.at[1])
    drain(gbuf.at[other_half], m_ss.at[0])
    drain(ubuf.at[other_half], m_ss.at[1])

    def part(mats, chunks, blocks):
        return out.at[pl.ds(0, mats), pl.ds(0, chunks * R), pl.ds(0, blocks * LANES)]

    for ref, sem in [
        (part(1, na - NB, NY * NZ), end_s.at[0]), (part(1, nd, 2 * NZ), end_s.at[1]), (part(2, NB, NY * NZ), o_sem),
        (a_raw, a_ss.at[RAW]), (a_x, a_ss.at[XSUM]), (a_t, a_ss.at[TREE]), (a_u, a_ss.at[TREE + 1]),
        (a_r.at[:, 3, 0], b_ss.at[RING + 3]), (a_qx, b_ss.at[MID]),
        (part(1, na - NB, NZ - 1), a_ss.at[FIRST]), (part(1, na - NB, (NY - 1) * NZ), a_ss.at[SECOND]),
        (part(1, na - NB, NY * NZ), a_ss.at[LAST]),
        (b_w.at[:, 0, 0, 0], b_ss.at[FIRST]), (b_w.at[:, 0, pl.ds(0, NY - 1)], b_ss.at[SECOND]),
        (b_w.at[:, 0], b_ss.at[LAST + 3]),
        (d_raw, d_ss.at[RAW]), (d_r.at[:, 3, 0], d_ss.at[RING + 3]), (d_qy, d_ss.at[MID]),
        (part(1, nd, NZ - 1), d_ss.at[FIRST]), (part(1, nd, NZ), d_ss.at[SECOND]),
        (part(2, nd, 2 * NZ), d_ss.at[LAST]), (part(1, nd, 2 * NZ), d_ss.at[LAST + 1]),
    ]:
        drain(ref, sem)
    for k in range(3):
        drain(a_r.at[:, k], b_ss.at[RING + k])
        drain(b_w.at[:, pl.ds(0, 2)], b_ss.at[LAST + k])
        drain(d_r.at[:, k], d_ss.at[RING + k])


def per_device(local, outer, momentum, swa, tokens, step_no):
    mats, rows, width = outer.shape
    nd = ND
    na = rows // R - nd
    f32, bf16, i32 = jnp.float32, jnp.bfloat16, jnp.int32
    vmem, dma = pltpu.VMEM, pltpu.SemaphoreType.DMA
    wide = NZ * LANES
    scratch = [
        vmem((na, NY - 1, mats, R, wide), bf16),
        vmem((mats, na * R, wide), bf16),
        vmem((mats, na * R, wide), bf16),
        vmem((na - NB, mats, NZ, R, LANES), f32),
        vmem((na - NB, NZ, R, LANES), f32),
        vmem((na - NB, 3, R, LANES), f32),
        vmem((na - NB, 4, R, LANES), f32),
        vmem((na - NB, R, LANES), bf16),
        vmem((NB, NZ, mats, R, LANES), f32),
        vmem((NB, 4, 2, mats, R, LANES), f32),
        vmem((NB, mats, R, LANES), f32),
        vmem((NB, R, LANES), f32),
        vmem((NB, NZ, NY, NX, R, LANES), bf16),
        vmem((NB, mats, R, width), bf16),
        vmem((nd, R, width), bf16),
        vmem((nd * R, width), bf16),
        vmem((nd * R, width), bf16),
        vmem((nd, NZ, NY, R, LANES), f32),
        vmem((nd, 4, 2, NY, R, LANES), f32),
        vmem((nd, NY, R, LANES), f32),
        vmem((nd, NY - 1, R, LANES), f32),
        vmem((nd, R, LANES), bf16),
        vmem((NY + 1, 8, LANES), i32),
        vmem((NZ, 8, LANES), i32),
        vmem((2, 8, LANES), i32),
        vmem((8, LANES), f32),
        vmem((LANES, rows), f32),
        vmem((LANES, rows), f32),
        vmem((rows, LANES), f32),
        vmem((rows, LANES), f32),
        vmem((rows, LANES), f32),
        vmem((rows, LANES), bf16),
        dma((9,)), dma((12,)), dma((na, 8)), dma((NB, 4)), dma((10,)), dma((nd, 9)),
        dma((3,)), dma((3,)), dma((2,)), dma((2,)), dma((7,)), dma, dma((2, 4)), dma((2,)),
    ]
    anywhere = pl.BlockSpec(memory_space=pl.ANY)
    in_hbm = pl.BlockSpec(memory_space=pltpu.HBM)
    in_smem = pl.BlockSpec(memory_space=pltpu.SMEM)
    turned = jax.ShapeDtypeStruct((mats, LANES // 2, rows), f32)
    shapes = (jax.ShapeDtypeStruct(outer.shape, bf16), turned, turned)
    results = pl.pallas_call(
        functools.partial(kernel, na, nd, rows),
        out_shape=shapes,
        in_specs=[in_hbm] * 3 + [in_smem],
        out_specs=(anywhere,) * 3,
        scratch_shapes=scratch,
        compiler_params=pltpu.CompilerParams(
            collective_id=0, has_side_effects=True, vmem_limit_bytes=47 * 2**20
        ),
    )(local, outer, jnp.swapaxes(momentum, 1, 2), tokens)
    new_weights, grad, updated = results
    grad, updated = jnp.swapaxes(grad, 1, 2), jnp.swapaxes(updated, 1, 2)
    divisor = step_no[0].astype(f32) + 1.0
    return new_weights, 0.9 * momentum + grad, swa + (updated - swa) / divisor


def solution(mesh):
    return jax.shard_map(
        per_device,
        mesh=mesh,
        in_specs=(
            P("rep", None, "fsdp", None),
            P(None, "fsdp", None),
            P(None, "fsdp", "rep"),
            P(None, "fsdp", "rep"),
            P("rep"),
            P(),
        ),
        out_specs=(P(None, "fsdp", None), P(None, "fsdp", "rep"), P(None, "fsdp", "rep")),
        check_vma=False,
    )
```

```python
import functools

import jax
import jax.numpy as jnp
from jax import lax
from jax.experimental import pallas as pl
from jax.experimental.pallas import tpu as pltpu
from jax.sharding import PartitionSpec as P

MESH = pl.DeviceIdType.MESH
NY, NZ, NX = 4, 8, 2
LANES = 128
R = 16
AHEAD = 3
NB = 4
ND = 6
A_AT = (0, 1, 2, 4, 5, 7)
B_AT = (0, 1, 3, 4, 5, 6, 8, 10, 12, 13, 15, 17)
D_AT = (0, 1, 3, 4, 5, 7, 9, 11, 13)
ORDER = (
    ("D", 2), ("B", 2), ("A", 0), ("B", 11), ("B", 10), ("B", 8), ("D", 7), ("A", 3), ("D", 6), ("D", 8), ("D", 3), ("B", 3), ("D", 0), ("D", 5), ("B", 9), ("B", 4), ("A", 5), ("D", 4), ("B", 0), ("A", 1), ("B", 5), ("B", 6), ("B", 7), ("A", 4), ("D", 1), ("A", 2), ("B", 1),
)
RAW, RING, MID, FIRST, SECOND, LAST = 0, 1, 5, 6, 7, 8
XSUM, TREE = 1, 2


def kernel(
    na, nd, rows,
    local, outer, mom_t, tokens,
    out, grad_t, upd_t,
    a_raw, a_own, a_out, a_p, a_x, a_t, a_u, a_v, b_p, a_r, a_q, a_qx, b_w, b_stage,
    d_raw, d_own, d_out, d_p, d_r, d_q, d_qy, d_v,
    cnt, cnt_z, cnt_x, total, gbuf, ubuf, mfull, gfull, ufull, ofull,
    a_ss, b_ss, a_rs, b_rs, d_ss, d_rs, c_ss, c_rs, m_ss, m_rs, l_sem, o_sem, v_sem, end_s,
):
    f32, bf16 = jnp.float32, jnp.bfloat16
    rep, fsdp = lax.axis_index("rep"), lax.axis_index("fsdp")
    y, z, x = rep // (NZ * NX), (rep // NX) % NZ, rep % NX
    other = 1 - x
    d_row = na * R

    def at(yy, zz, xx):
        return ((lax.rem(yy + 2 * NY, NY) * NZ + lax.rem(zz + 2 * NZ, NZ)) * NX + xx, fsdp)

    def zi(k):
        return lax.rem(z + k + 2 * NZ, NZ)

    def yi(k):
        return lax.rem(y + k + 2 * NY, NY)

    def send(src, dst, ss, rs, where):
        pltpu.make_async_remote_copy(
            src_ref=src, dst_ref=dst, send_sem=ss, recv_sem=rs, device_id=where, device_id_type=MESH
        ).start()

    def drain(ref, sem):
        pltpu.make_async_copy(ref, ref, sem).wait()

    partner = at(y, z, other)
    y_peers = [at(y + k, z, x) for k in range(1, NY)]
    z_peers = [at(y, z + k, x) for k in range(1, NZ)]

    def a_rows(c):
        return pl.ds(pl.multiple_of(c * R, R), R)

    def d_rows(c):
        return pl.ds(pl.multiple_of(d_row + c * R, R), R)

    def lanes(block):
        return pl.ds(block * LANES, LANES)

    def cnt_f(k):
        return cnt[k, 0:1, :].astype(f32)

    half = pl.ds(pl.multiple_of(x * (LANES // 2), LANES // 2), LANES // 2)
    other_half = pl.ds(pl.multiple_of(other * (LANES // 2), LANES // 2), LANES // 2)
    ycols = pl.ds(pl.multiple_of(y * (NZ * LANES), NZ * LANES), NZ * LANES)
    cols = pl.ds(pl.multiple_of((y * NZ + z) * LANES, LANES), LANES)
    arows, drows = pl.ds(0, na * R), pl.ds(d_row, nd * R)
    loads = [
        pltpu.make_async_copy(local.at[0, :, arows, ycols], a_own, l_sem.at[1]),
        pltpu.make_async_copy(outer.at[:, arows, ycols], a_out, l_sem.at[2]),
        pltpu.make_async_copy(local.at[0, x, drows, :], d_own, l_sem.at[3]),
        pltpu.make_async_copy(outer.at[x, drows, :], d_out, l_sem.at[4]),
    ]
    late_loads = [
        pltpu.make_async_copy(outer.at[x, :, cols], ofull, l_sem.at[0]),
        pltpu.make_async_copy(mom_t.at[x], gbuf.at[half], l_sem.at[5]),
    ]
    for load in loads + late_loads:
        load.start()
    cnt[0] = jnp.full((8, LANES), tokens[0], jnp.int32)

    barrier = pltpu.get_barrier_semaphore()
    peers = y_peers + z_peers + [partner]
    for peer in peers:
        pl.semaphore_signal(barrier, inc=1, device_id=peer, device_id_type=MESH)
    pl.semaphore_wait(barrier, len(peers))

    def send_raw(c):
        @pl.when(c < na)
        def _():
            for k in (2, 1, 3):
                theirs = pl.ds(pl.multiple_of(yi(k) * (NZ * LANES), NZ * LANES), NZ * LANES)
                send(
                    local.at[0, :, a_rows(c), theirs], a_raw.at[c, k - 1],
                    a_ss.at[RAW], a_rs.at[c, RAW], y_peers[k - 1],
                )

        @pl.when(c < nd)
        def _():
            send(local.at[0, other, d_rows(c), :], d_raw.at[c], d_ss.at[RAW], d_rs.at[c, RAW], partner)

    def ring_stage(stage, c, sign, p, r, ss, rs):
        up, down = at(y, z + sign, x), at(y, z - sign, x)

        def step(k, long, short):
            send(long, r.at[c, k, 0], ss.at[RING + k], rs.at[c, RING + k], up)
            if k < 3:
                send(short, r.at[c, k, 1], ss.at[RING + k], rs.at[c, RING + k], down)

        if stage == 0:
            step(0, p.at[c, zi(4 * sign)], p.at[c, zi(-3 * sign)])
            return
        k = stage - 1
        came = r.at[c, k] if k < 3 else r.at[c, k, 0]
        drain(came, rs.at[c, RING + k])
        if k < 3:
            r[c, k, 0] += p[c, zi((3 - k) * sign)]
            if k < 2:
                r[c, k, 1] += p[c, zi(-(2 - k) * sign)]
            step(k + 1, r.at[c, k, 0], r.at[c, k, 1])

    def update(rws, pg_sum):
        o = ofull[rws, :].astype(f32)
        pg = pg_sum / total[0:1, :]
        upd = o - 0.7 * (pg + 0.9 * (0.9 * mfull[rws, :] + pg))
        gfull[rws, :] = pg
        ufull[rws, :] = upd
        return upd.astype(bf16)

    def a_sums(c, keep):
        drain(a_raw.at[c], a_rs.at[c, RAW])
        for zz in range(NZ):
            for m in range(2):
                o = a_out[m, a_rows(c), lanes(zz)].astype(f32)
                acc = cnt_f(0) * (o - a_own[m, a_rows(c), lanes(zz)].astype(f32))
                for k in range(1, NY):
                    acc += cnt_f(k) * (o - a_raw[c, k - 1, m, :, lanes(zz)].astype(f32))
                keep(m, zz, acc)

    def a_stage_fn(stage, c):
        e = c - NB
        sign = 1 - 2 * (c % 2)

        def sems(k):
            return a_ss.at[k], a_rs.at[c, k]

        def landed(ref, k):
            drain(ref, a_rs.at[c, k])

        if stage == 0:
            def keep(m, zz, acc):
                a_p[e, m, zz] = acc

            a_sums(c, keep)
            send(a_p.at[e, other], a_x.at[e], *sems(XSUM), partner)
        elif stage == 1:
            landed(a_x.at[e], XSUM)
            a_x[e] += a_p[e, x]
            send(a_x.at[e, zi(4 * sign)], a_t.at[e, 0], *sems(TREE), at(y, z + 2 * sign, x))
            send(a_x.at[e, zi(3 * sign)], a_t.at[e, 1], *sems(TREE), at(y, z + sign, x))
            send(a_x.at[e, zi(-3 * sign)], a_t.at[e, 2], *sems(TREE), at(y, z - sign, x))
        elif stage == 2:
            landed(a_t.at[e], TREE)
            a_t[e, 0] += a_t[e, 1] + a_x[e, zi(2 * sign)]
            a_t[e, 2] += a_x[e, zi(-2 * sign)]
            send(a_t.at[e, 0], a_u.at[e, 0], *sems(TREE + 1), at(y, z + 2 * sign, x))
            send(a_t.at[e, 2], a_u.at[e, 1], *sems(TREE + 1), at(y, z - 2 * sign, x))
            send(a_x.at[e, zi(sign)], a_u.at[e, 2], *sems(TREE + 1), at(y, z + sign, x))
            send(a_x.at[e, zi(-sign)], a_u.at[e, 3], *sems(TREE + 1), at(y, z - sign, x))
        elif stage == 3:
            landed(a_u.at[e], TREE + 1)
            a_v[e] = update(a_rows(c), a_x[e, z] + ((a_u[e, 0] + a_u[e, 1]) + (a_u[e, 2] + a_u[e, 3])))
            place = out.at[x, a_rows(c), cols]
            pltpu.make_async_copy(a_v.at[e], place, v_sem.at[0, c % 4]).start()
            for k in (4, 3, 5, 2, 6, 1, 7):
                send(a_v.at[e], place, *sems(FIRST), z_peers[k - 1])
        elif stage == 4:
            landed(out.at[x, a_rows(c), pl.ds(0, (NZ - 1) * LANES)], FIRST)
            drain(a_v.at[e], v_sem.at[0, c % 4])
            place = out.at[x, a_rows(c), ycols]
            for k in (2, 1, 3):
                send(place, place, *sems(SECOND), y_peers[k - 1])
        else:
            landed(out.at[x, a_rows(c), pl.ds(0, (NY - 1) * NZ * LANES)], SECOND)
            place = out.at[x, a_rows(c), :]
            send(place, place, a_ss.at[LAST], end_s.at[0], partner)

    def b_stage_fn(stage, c):
        sign = 1 - 2 * (c % 2)
        up, down = at(y, z + sign, x), at(y, z - sign, x)

        def sems(k):
            return b_ss.at[k], a_rs.at[c, k]

        def landed(ref, k):
            drain(ref, a_rs.at[c, k])

        def step(k):
            long, short = b_w.at[c, zi(-k * sign)], b_w.at[c, zi(k * sign)]
            send(long, long, b_ss.at[LAST + k], b_rs.at[c, k], up)
            if k < 3:
                send(short, short, b_ss.at[LAST + k], b_rs.at[c, k], down)

        ring = functools.partial(ring_stage, c=c, sign=sign, p=b_p, r=a_r, ss=b_ss, rs=a_rs)
        if stage == 0:

            def keep(m, zz, acc):
                b_p[c, zz, m] = acc

            a_sums(c, keep)
            ring(0)
        elif stage <= 3:
            ring(stage)
        elif stage == 4:
            ring(4)
            a_q[c] = b_p[c, z] + a_r[c, 3, 0] + a_r[c, 2, 1]
            send(a_q.at[c, other], a_qx.at[c], *sems(MID), partner)
        elif stage == 5:
            landed(a_qx.at[c], MID)
            mine = b_w.at[c, z, y, x]
            mine[...] = update(a_rows(c), a_q[c, x] + a_qx[c])
            send(mine, mine, *sems(FIRST), partner)
        elif stage == 6:
            landed(b_w.at[c, z, y, other], FIRST)
            mine = b_w.at[c, z, y]
            for k in (2, 1, 3):
                send(mine, mine, *sems(SECOND), y_peers[k - 1])
        elif stage == 7:
            landed(b_w.at[c, z, pl.ds(0, NY - 1)], SECOND)
            step(0)
        else:
            k = stage - 8
            came = b_w.at[c, pl.ds(0, 2 if k < 3 else 1)]
            drain(came, b_rs.at[c, k])
            if k < 3:
                step(k + 1)
            else:
                for yy in range(NY):
                    for zz in range(NZ):
                        for m in range(2):
                            b_stage[c, m, :, lanes(yy * NZ + zz)] = b_w[c, zz, yy, m]
                pltpu.make_async_copy(b_stage.at[c], out.at[:, a_rows(c), :], o_sem).start()

    def d_stage_fn(stage, c):
        ring = functools.partial(ring_stage, c=c, sign=2 * (c % 2) - 1, p=d_p, r=d_r, ss=d_ss, rs=d_rs)

        def sems(k):
            return d_ss.at[k], d_rs.at[c, k]

        def landed(ref, k):
            drain(ref, d_rs.at[c, k])

        if stage == 0:
            landed(d_raw.at[c], RAW)
            own = pl.ds(pl.multiple_of(c * R, R), R)
            for yy in range(NY):
                for zz in range(NZ):
                    sl = lanes(yy * NZ + zz)
                    o = d_out[own, sl].astype(f32)
                    mine = cnt_f(0) * (o - d_own[own, sl].astype(f32))
                    d_p[c, zz, yy] = mine + cnt_f(NY) * (o - d_raw[c, :, sl].astype(f32))
            ring(0)
        elif stage <= 3:
            ring(stage)
        elif stage == 4:
            ring(4)
            d_q[c] = d_p[c, z] + d_r[c, 3, 0] + d_r[c, 2, 1]
            for k in (2, 1, 3):
                send(d_q.at[c, yi(k)], d_qy.at[c, k - 1], *sems(MID), y_peers[k - 1])
        elif stage == 5:
            landed(d_qy.at[c], MID)
            d_v[c] = update(d_rows(c), d_q[c, y] + d_qy[c, 0] + d_qy[c, 1] + d_qy[c, 2])
            place = out.at[x, d_rows(c), cols]
            pltpu.make_async_copy(d_v.at[c], place, v_sem.at[1, c % 4]).start()
            for k in (4, 3, 5, 2, 6, 1, 7):
                send(d_v.at[c], place, *sems(FIRST), z_peers[k - 1])
        elif stage == 6:
            landed(out.at[x, d_rows(c), pl.ds(0, (NZ - 1) * LANES)], FIRST)
            drain(d_v.at[c], v_sem.at[1, c % 4])
            place = out.at[x, d_rows(c), ycols]
            send(place, place, *sems(SECOND), partner)
        elif stage == 7:
            landed(out.at[other, d_rows(c), ycols], SECOND)
            place = out.at[:, d_rows(c), ycols]
            for k in (1, 3):
                send(place, place, *sems(LAST), y_peers[k - 1])
        else:
            landed(out.at[:, d_rows(c), pl.ds(0, 2 * NZ * LANES)], LAST)
            for k, m in ((1, 0), (-1, 1)):
                theirs = pl.ds(pl.multiple_of(yi(-k) * (NZ * LANES), NZ * LANES), NZ * LANES)
                place = out.at[m, d_rows(c), theirs]
                send(place, place, d_ss.at[LAST + 1], end_s.at[1], at(y + k, z, x))

    send_raw(0)
    for k in range(1, NY):
        send(cnt.at[0], cnt.at[k], c_ss.at[0], c_rs.at[0], y_peers[k - 1])
    send(cnt.at[0], cnt.at[NY], c_ss.at[0], c_rs.at[0], partner)
    for c in range(1, AHEAD):
        send_raw(c)
    drain(cnt.at[pl.ds(0, NY)], c_rs.at[0])
    drain(cnt.at[pl.ds(0, NY)], c_ss.at[0])
    cnt_z[0] = cnt[0] + cnt[1] + cnt[2] + cnt[3]
    for k in range(1, NZ):
        send(cnt_z.at[0], cnt_z.at[k], c_ss.at[1], c_rs.at[1], z_peers[k - 1])
    for load in loads:
        load.wait()

    def slot(t, carry):
        @pl.when(t == 2)
        def _():
            drain(cnt_z.at[pl.ds(0, NZ - 1)], c_rs.at[1])
            drain(cnt_z.at[pl.ds(0, NZ - 1)], c_ss.at[1])
            acc = cnt_z[0]
            for k in range(1, NZ):
                acc += cnt_z[k]
            cnt_x[0] = acc
            send(cnt_x.at[0], cnt_x.at[1], c_ss.at[2], c_rs.at[2], partner)
            send(mom_t.at[other], gbuf.at[half], m_ss.at[0], m_rs.at[0], partner)

        @pl.when(t == 5)
        def _():
            drain(cnt_x.at[0], c_rs.at[2])
            drain(cnt_x.at[0], c_ss.at[2])
            total[...] = (cnt_x[0] + cnt_x[1]).astype(f32)
            drain(gbuf.at[other_half], m_rs.at[0])
            drain(gbuf.at[other_half], m_ss.at[0])
            for load in late_loads:
                load.wait()
            mfull[...] = gbuf[...].T

        for kind, stage in ORDER:
            if kind == "D":
                c, low, high, fn = t - D_AT[stage], 0, nd, d_stage_fn
            elif kind == "B":
                c, low, high, fn = t - B_AT[stage], 0, NB, b_stage_fn
            else:
                c, low, high, fn = t - A_AT[stage], NB, na, a_stage_fn
            pl.when((c >= low) & (c < high))(functools.partial(fn, stage, c))
        send_raw(t + AHEAD)

        @pl.when(t == max(na + A_AT[3], NB + B_AT[5], nd + D_AT[5]))
        def _():
            gbuf[...] = gfull[...].T
            ubuf[...] = ufull[...].T
            send(gbuf.at[other_half], grad_t.at[x], m_ss.at[0], m_rs.at[0], partner)
            send(ubuf.at[other_half], upd_t.at[x], m_ss.at[1], m_rs.at[1], partner)
            pltpu.make_async_copy(gbuf.at[half], grad_t.at[x], l_sem.at[5]).start()
            pltpu.make_async_copy(ubuf.at[half], upd_t.at[x], l_sem.at[6]).start()

        return carry

    lax.fori_loop(0, max(na + A_AT[-1], NB + B_AT[-1], nd + D_AT[-1]), slot, 0)
    pltpu.make_async_copy(gbuf.at[half], grad_t.at[x], l_sem.at[5]).wait()
    pltpu.make_async_copy(ubuf.at[half], upd_t.at[x], l_sem.at[6]).wait()
    drain(grad_t.at[other], m_rs.at[0])
    drain(upd_t.at[other], m_rs.at[1])
    drain(gbuf.at[other_half], m_ss.at[0])
    drain(ubuf.at[other_half], m_ss.at[1])

    def part(mats, chunks, blocks):
        return out.at[pl.ds(0, mats), pl.ds(0, chunks * R), pl.ds(0, blocks * LANES)]

    for ref, sem in [
        (part(2, NB, NY * NZ), o_sem),
        (a_raw, a_ss.at[RAW]), (a_x, a_ss.at[XSUM]), (a_t, a_ss.at[TREE]), (a_u, a_ss.at[TREE + 1]),
        (a_r.at[:, 3, 0], b_ss.at[RING + 3]), (a_qx, b_ss.at[MID]),
        (part(1, na - NB, NZ - 1), a_ss.at[FIRST]), (part(1, na - NB, (NY - 1) * NZ), a_ss.at[SECOND]),
        (part(1, na - NB, NY * NZ), a_ss.at[LAST]),
        (b_w.at[:, 0, 0, 0], b_ss.at[FIRST]), (b_w.at[:, 0, pl.ds(0, NY - 1)], b_ss.at[SECOND]),
        (b_w.at[:, 0], b_ss.at[LAST + 3]),
        (d_raw, d_ss.at[RAW]), (d_r.at[:, 3, 0], d_ss.at[RING + 3]), (d_qy, d_ss.at[MID]),
        (part(1, nd, NZ - 1), d_ss.at[FIRST]), (part(1, nd, NZ), d_ss.at[SECOND]),
        (part(2, nd, 2 * NZ), d_ss.at[LAST]), (part(1, nd, 2 * NZ), d_ss.at[LAST + 1]),
    ]:
        drain(ref, sem)
    for k in range(3):
        drain(a_r.at[:, k], b_ss.at[RING + k])
        drain(b_w.at[:, pl.ds(0, 2)], b_ss.at[LAST + k])
        drain(d_r.at[:, k], d_ss.at[RING + k])
    drain(part(1, na - NB, NY * NZ), end_s.at[0])
    drain(part(1, nd, 2 * NZ), end_s.at[1])


def per_device(local, outer, momentum, swa, tokens, step_no):
    mats, rows, width = outer.shape
    nd = ND
    na = rows // R - nd
    f32, bf16, i32 = jnp.float32, jnp.bfloat16, jnp.int32
    vmem, dma = pltpu.VMEM, pltpu.SemaphoreType.DMA
    wide = NZ * LANES
    scratch = [
        vmem((na, NY - 1, mats, R, wide), bf16),
        vmem((mats, na * R, wide), bf16),
        vmem((mats, na * R, wide), bf16),
        vmem((na - NB, mats, NZ, R, LANES), f32),
        vmem((na - NB, NZ, R, LANES), f32),
        vmem((na - NB, 3, R, LANES), f32),
        vmem((na - NB, 4, R, LANES), f32),
        vmem((na - NB, R, LANES), bf16),
        vmem((NB, NZ, mats, R, LANES), f32),
        vmem((NB, 4, 2, mats, R, LANES), f32),
        vmem((NB, mats, R, LANES), f32),
        vmem((NB, R, LANES), f32),
        vmem((NB, NZ, NY, NX, R, LANES), bf16),
        vmem((NB, mats, R, width), bf16),
        vmem((nd, R, width), bf16),
        vmem((nd * R, width), bf16),
        vmem((nd * R, width), bf16),
        vmem((nd, NZ, NY, R, LANES), f32),
        vmem((nd, 4, 2, NY, R, LANES), f32),
        vmem((nd, NY, R, LANES), f32),
        vmem((nd, NY - 1, R, LANES), f32),
        vmem((nd, R, LANES), bf16),
        vmem((NY + 1, 8, LANES), i32),
        vmem((NZ, 8, LANES), i32),
        vmem((2, 8, LANES), i32),
        vmem((8, LANES), f32),
        vmem((LANES, rows), f32),
        vmem((LANES, rows), f32),
        vmem((rows, LANES), f32),
        vmem((rows, LANES), f32),
        vmem((rows, LANES), f32),
        vmem((rows, LANES), bf16),
        dma((9,)), dma((12,)), dma((na, 8)), dma((NB, 4)), dma((10,)), dma((nd, 9)),
        dma((3,)), dma((3,)), dma((2,)), dma((2,)), dma((7,)), dma, dma((2, 4)), dma((2,)),
    ]
    anywhere = pl.BlockSpec(memory_space=pl.ANY)
    in_hbm = pl.BlockSpec(memory_space=pltpu.HBM)
    in_smem = pl.BlockSpec(memory_space=pltpu.SMEM)
    turned = jax.ShapeDtypeStruct((mats, LANES // 2, rows), f32)
    shapes = (jax.ShapeDtypeStruct(outer.shape, bf16), turned, turned)
    results = pl.pallas_call(
        functools.partial(kernel, na, nd, rows),
        out_shape=shapes,
        in_specs=[in_hbm] * 3 + [in_smem],
        out_specs=(anywhere,) * 3,
        scratch_shapes=scratch,
        compiler_params=pltpu.CompilerParams(
            collective_id=0, has_side_effects=True, vmem_limit_bytes=47 * 2**20
        ),
    )(local, outer, jnp.swapaxes(momentum, 1, 2), tokens)
    new_weights, grad, updated = results
    grad, updated = jnp.swapaxes(grad, 1, 2), jnp.swapaxes(updated, 1, 2)
    divisor = step_no[0].astype(f32) + 1.0
    return new_weights, 0.9 * momentum + grad, swa + (updated - swa) / divisor


def solution(mesh):
    return jax.shard_map(
        per_device,
        mesh=mesh,
        in_specs=(
            P("rep", None, "fsdp", None),
            P(None, "fsdp", None),
            P(None, "fsdp", "rep"),
            P(None, "fsdp", "rep"),
            P("rep"),
            P(),
        ),
        out_specs=(P(None, "fsdp", None), P(None, "fsdp", "rep"), P(None, "fsdp", "rep")),
        check_vma=False,
    )
```
